256 devices in a mesh: slab: 16 (over x_lo, y, core), blk: 16 (over z, x_hi).
Axes of the slice: x: 4 (x_hi: 2, x_lo: 2; x = x_hi * 2 + x_lo), y: 4, z: 8, core: 2. Of those that a mesh axis runs over, the one named last changes fastest.
Arguments:
- amplitude: float32 [1024, 2048], P('blk'), may hold values from -6 to 6
- integrals: float32 [2048, 16, 16, 800], P(None, 'slab', 'blk'), may hold values from -0.375 to 0.375
- row_irrep: int32 [128], replicated, may hold values from 0 to 7
- cd_irrep: int32 [16], replicated, may hold values from 0 to 7
- a_irrep: int32 [16, 16], replicated, may hold values from 0 to 7
- owner: int32 [128, 1], replicated, may hold values from 0 to 15; in each aligned block of 128 rows (0 to 127, 128 to 255, ...) at most 16 rows name the same one
Outputs:
- owned: float32 [2048, 16, 16, 800], P('slab', None, 'blk')
The draws below stay inside these ranges and needn't reach their ends.
Inputs may be any that keep to these rules, and one draw needn't show every extreme that they name: `owner`: no slab index owns more than 16 tiles, and some slab index owns exactly 16.
All inputs are finite; a program needn't handle non-finite values.
Results may differ from the reference program's by a relative error of at most 0.000071.
Values sent between devices are 32-bit elements; how exact they have to be, the bound alone decides.
A program may use at most 128 MiB of HBM per device.

```python
import math
import jax
import jax.numpy as jnp
import numpy as np
from jax import lax

NVIR = 800
CDPAIRS = 2048
CD_TILE = 128
ROW_TILE = 8
VBLOCK = 100
PAIRS = 1024
TILES = 128
CAPACITY = 16
KTILES = 16
SLABS = 16
SLAB_A = 16
N_SLAB = 16


def plant(array, own_key, smallest, largest):
    place = [jax.random.randint(jax.random.fold_in(own_key, axis), (), 0, length) for axis, length in enumerate(array.shape)]
    longest = array.shape.index(max(array.shape))
    neighbour = place[:longest] + [(place[longest] + 1) % array.shape[longest]] + place[longest + 1:]
    return array.at[tuple(place)].set(smallest).at[tuple(neighbour)].set(largest)


def block_levels(stream_key, shape, shards, smallest, top_value):
    def one(dim, shards_of):
        steps = jax.random.uniform(jax.random.fold_in(jax.random.fold_in(stream_key, 6), dim), (shards_of,), jnp.float32, smallest / len(shards), top_value / len(shards))
        return jnp.repeat(jnp.exp(steps), shape[dim] // shards_of).reshape((-1,) + (1,) * (len(shape) - dim - 1))

    factor_of = one(*shards[0])
    for cut in shards[1:]:
        factor_of = factor_of * one(*cut)
    return factor_of


def assign_block(rng, own, number, rows, count, top, reach, slope):
    order = jax.random.permutation(rng, count)
    crowded, common = portions_of(count, rows * top, reach, slope, True), portions_of(count, rows * top, reach, slope, False)
    places = jnp.arange(count)

    def named(lengths, rotation):
        used = int((lengths > 0).sum())
        fixed = max(1, used // 4)
        shifted = fixed + (places - fixed + rotation * (used - fixed)) % max(1, count - fixed)
        return jnp.zeros((count,), jnp.int32).at[order[jnp.where(places < fixed, places, shifted)]].set(jnp.asarray(lengths, jnp.int32))

    lengths = jnp.where(number % 4 == 0, named(crowded, number // 4), named(common, number - number // 4 - 1))
    mixed = jax.random.permutation(jax.random.fold_in(own, 3), count)
    donor, sink = mixed[0:count // 2 * 2:2], mixed[1:count // 2 * 2:2]
    slack = jnp.minimum(lengths[donor] - 1, reach - lengths[sink]) // 2
    slack = jnp.where((donor == order[0]) | (sink == order[0]) | (lengths[sink] == 0), 0, jnp.maximum(slack, 0))
    shifted = jax.random.randint(jax.random.fold_in(own, 4), (count // 2,), 0, 1 << 20) % (slack + 1)
    lengths = lengths.at[donor].add(-shifted).at[sink].add(shifted)
    members = jnp.searchsorted(jnp.cumsum(lengths), jnp.arange(rows * top), side="right").astype(jnp.int32)
    grid = members.reshape(top, rows).T
    grid = grid[jax.random.permutation(jax.random.fold_in(own, 1), rows)]
    rotation = jax.random.randint(jax.random.fold_in(own, 2), (rows, 1), 0, top)
    return jnp.take_along_axis(grid, (jnp.arange(top)[None, :] + rotation) % top, axis=1)


def portions_of(count, total, limit, skew, full):
    weights = [(1 << 20) // math.isqrt(rank ** skew) + 1 for rank in range(1, count + 1)]
    largest = limit if full else min(limit, max(-(-total // count), total * weights[0] // sum(weights)))
    least = 1 if total - largest >= count - 1 else 0
    counts, spare = [largest] + [least] * (count - 1), total - largest - least * (count - 1)
    while spare > 0:
        movable = [i for i in range(1, count) if counts[i] < largest] or [i for i in range(1, count) if counts[i] < limit]
        whole, budget = sum([weights[i] for i in movable]), spare
        for i in movable:
            addition = min(limit - counts[i], max(1, budget * weights[i] // whole), spare)
            counts[i] = counts[i] + addition
            spare = spare - addition
    return np.array(counts)


def normal_values(stream_key, dims, width, bound, shards=(), held_as=jnp.bfloat16):
    drawn = width * jax.random.normal(stream_key, dims, jnp.float32)
    if shards:
        drawn = drawn * block_levels(stream_key, dims, shards, -0.22, 0.18)
    return jnp.clip(drawn, -bound, bound).astype(held_as)


def setup_inputs(seed: int = 0) -> dict:
    arg_keys = jax.random.split(jax.random.key(seed), 7)
    amplitude = normal_values(arg_keys[0], (PAIRS, CDPAIRS), 1.0, 6.0, ((0, 16),), jnp.float32)
    integrals = normal_values(arg_keys[1], (CDPAIRS, SLABS, SLAB_A, NVIR), (CDPAIRS // 8) ** -0.5, 0.375, ((1, 16), (2, 16)), jnp.float32)
    row_irrep = plant(jax.random.randint(arg_keys[2], (TILES,), 0, 8), jax.random.fold_in(arg_keys[2], 1), 0, 7).astype(jnp.int32)
    cd_irrep = plant(jax.random.randint(arg_keys[3], (KTILES,), 0, 8), jax.random.fold_in(arg_keys[3], 1), 0, 7).astype(jnp.int32)
    a_irrep = plant(jax.random.randint(arg_keys[4], (SLABS, SLAB_A), 0, 8), jax.random.fold_in(arg_keys[4], 1), 0, 7).astype(jnp.int32)
    owner_keys = jax.random.split(jax.random.fold_in(arg_keys[5], 1), TILES // TILES)
    owner_turns = jax.random.permutation(jax.random.fold_in(arg_keys[5], 3), TILES // TILES)
    owner = jax.vmap(lambda own, number: assign_block(jax.random.fold_in(arg_keys[5], 2), own, number, TILES, N_SLAB, 1, CAPACITY, 2))(owner_keys, owner_turns).reshape((TILES, 1))
    return {"amplitude": amplitude, "integrals": integrals, "row_irrep": row_irrep, "cd_irrep": cd_irrep, "a_irrep": a_irrep, "owner": owner}


def slot_sources(owner, n_slab, capacity):
    owners = owner[:, 0]
    ntiles = owners.shape[0]
    onehot = (owners[:, None] == jnp.arange(n_slab, dtype=jnp.int32)[None, :]).astype(jnp.int32)
    before = jnp.cumsum(onehot, axis=0) - onehot
    rank = jnp.sum(before * onehot, axis=1)
    target = owners * capacity + rank
    slots = jnp.arange(n_slab * capacity, dtype=jnp.int32)
    match = target[None, :] == slots[:, None]
    source = jnp.sum(jnp.where(match, jnp.arange(ntiles, dtype=jnp.int32)[None, :], 0), axis=1).astype(jnp.int32)
    filled = jnp.any(match, axis=1)
    return match, source, filled


def reference(amplitude, integrals, row_irrep, cd_irrep, a_irrep, owner):
    labels = jnp.take(row_irrep, jnp.arange(PAIRS, dtype=jnp.int32) // ROW_TILE)
    column_labels = jnp.take(cd_irrep, jnp.arange(CDPAIRS, dtype=jnp.int32) // CD_TILE)
    vir_labels = (jnp.arange(NVIR, dtype=jnp.int32) // VBLOCK).astype(jnp.int32)
    coupled = jnp.where(labels[:, None] == column_labels[None, :], amplitude, 0.0)
    flat = integrals.reshape(CDPAIRS, SLABS * SLAB_A * NVIR)
    product = jnp.dot(coupled, flat, precision=lax.Precision.HIGHEST, preferred_element_type=jnp.float32)
    product = product.reshape(PAIRS, SLABS, SLAB_A, NVIR)
    pair_labels = jnp.bitwise_xor(a_irrep[:, :, None], vir_labels[None, None, :])
    ladder = jnp.where(labels[:, None, None, None] == pair_labels[None], product, 0.0)
    match, source, filled = slot_sources(owner, SLABS, CAPACITY)
    tiles = ladder.reshape(TILES, ROW_TILE, SLABS, SLAB_A, NVIR)
    owned = jnp.where(filled[:, None, None, None, None], jnp.take(tiles, source, axis=0), 0.0)
    return owned.reshape(SLABS * CAPACITY * ROW_TILE, SLABS, SLAB_A, NVIR)
```

```python
import functools

import jax
import jax.numpy as jnp
from jax import lax
from jax.experimental import pallas as pl
from jax.experimental.pallas import tpu as pltpu
from jax.sharding import PartitionSpec as P

IRREPS = 8
CD_TILE = 128
ROW_TILE = 8
TILES = 128
KT = 16
OWN_TILES = 8
SLOTS = 32
CAP = 16
VB = 100
VP = 104
ZEROT = 128
DUMPT = 129
PT = 136
T_LST = 0
T_OFF = 1024
T_KL = 1152
T_SRC = 1280
T_NR = 1536
T_NK = 1544
T_FIT = 1552
T_NO = 1560
T_SIZE = 2048

MESH = pl.DeviceIdType.MESH
F32 = jnp.float32
BF16 = jnp.bfloat16


def prep_kernel(row, cd, own, amp, comp, tab):
    me = lax.axis_index("blk")
    for i in range(IRREPS):
        tab[T_NR + i] = 0
        tab[T_NK + i] = 0
    for i in range(16):
        tab[T_NO + i] = 0
    for k in range(KT):
        lab = cd[k]
        kap = tab[T_NK + lab]
        tab[T_KL + lab * KT + kap] = k
        tab[T_NK + lab] = kap + 1
    labs = [cd[k] for k in range(KT)]
    j = jnp.int32(0)
    for t in range(OWN_TILES):
        lab = row[me * OWN_TILES + t]
        for k in range(KT):
            jc = jnp.minimum(j, SLOTS)
            comp[pl.ds(pl.multiple_of(jc * 8, 8), 8), :] = amp[t * 8:(t + 1) * 8, k * 128:(k + 1) * 128]
            j = j + jnp.where(labs[k] == lab, 1, 0)

    def clear(i, c):
        tab[T_SRC + i] = ZEROT
        return c

    lax.fori_loop(0, 256, clear, 0, unroll=16)

    def group(g, most):
        acc = jnp.int32(0)
        for t in range(OWN_TILES):
            r = g * OWN_TILES + t
            lab = row[r]
            p = tab[T_NR + lab]
            tab[T_LST + lab * TILES + p] = r
            tab[T_NR + lab] = p + 1
            o = own[r]
            q = tab[T_NO + o]
            tab[T_SRC + o * CAP + q] = r
            tab[T_NO + o] = q + 1
            tab[T_OFF + r] = g * SLOTS + acc
            acc = acc + tab[T_NK + lab]
        return jnp.maximum(most, acc)

    most = lax.fori_loop(0, TILES // OWN_TILES, group, jnp.int32(0))
    tab[T_FIT] = jnp.where(most <= SLOTS, 1, 0)


def prep(row, cd, own, amp):
    smem = pl.BlockSpec(memory_space=pltpu.SMEM)
    vmem = pl.BlockSpec(memory_space=pltpu.VMEM)
    return pl.pallas_call(
        prep_kernel,
        out_shape=(
            jax.ShapeDtypeStruct(((SLOTS + 1) * 8, 128), F32),
            jax.ShapeDtypeStruct((T_SIZE,), jnp.int32),
        ),
        in_specs=[smem, smem, smem, vmem],
        out_specs=(vmem, smem),
        name="prep",
    )(row, cd, own, amp)


ORDER = (0, 1, 7, 2, 6, 3, 5, 4)


def gather_kernel(cd, airr, comp, integ, g, w, raw, loc_sem, raw_sem, s1, r1, s2, r2, s3, r3):
    slab = lax.axis_index("slab")
    blk = lax.axis_index("blk")
    c = slab % 2
    y = (slab // 2) % 4
    xl = slab // 8
    z = blk // 2
    xh = blk % 2
    x = xh * 2 + xl
    pos = (1 - c) * x + c * y

    def dev(x_, y_, z_, c_):
        return {"slab": (x_ % 2) * 8 + y_ * 2 + c_, "blk": z_ * 2 + x_ // 2}

    raw_copy = pltpu.make_async_copy(integ, raw, raw_sem)
    raw_copy.start()

    col = [dev(x, y, (z + d) % 8, c) for d in range(8)]
    cross = [dev(3 - x, y, (z + d) % 8, c) for d in range(8)]
    ring = [None] + [dev((x + (1 - c) * j) % 4, (y + c * j) % 4, z, c) for j in range(1, 4)]
    twin = dev(x, y, z, 1 - c)

    barrier = pltpu.get_barrier_semaphore()
    peers = col[1:] + cross + ring[1:] + [twin]
    for peer in peers:
        pl.semaphore_signal(barrier, inc=1, device_id=peer, device_id_type=MESH)

    def rows(c_, p_):
        return pl.ds(pl.multiple_of(c_ * 128 + p_ * 32, 32), 32)

    mine = pltpu.make_async_copy(comp.at[rows(c, pos)], g.at[blk, rows(c, pos)], loc_sem)
    mine.start()
    pl.semaphore_wait(barrier, len(peers))

    cross_pos = (1 - c) * (3 - x) + c * y
    first = []
    for d in ORDER:
        if d != 0:
            cp = pltpu.make_async_remote_copy(
                src_ref=comp.at[rows(c, pos)], dst_ref=g.at[blk, rows(c, pos)],
                send_sem=s1.at[0, d], recv_sem=r1.at[0, d],
                device_id=col[d], device_id_type=MESH)
            cp.start()
            first.append(cp)
        cp = pltpu.make_async_remote_copy(
            src_ref=comp.at[rows(c, cross_pos)], dst_ref=g.at[blk, rows(c, cross_pos)],
            send_sem=s1.at[1, d], recv_sem=r1.at[1, d],
            device_id=cross[d], device_id_type=MESH)
        cp.start()
        first.append(cp)

    raw_copy.wait()
    a = airr[slab, blk]

    def weights(k):
        beta = cd[k] ^ a
        odd = beta & 1
        start = beta * 12 + beta // 2
        block = jnp.concatenate([raw[start + i, :, k * 128:(k + 1) * 128] for i in range(VP // 8)], axis=0)
        moved = jnp.concatenate([block[4:], block[:4]], axis=0)
        block = jnp.where(odd == 1, moved, block)
        block = jnp.concatenate([block, jnp.zeros((128 - VP, 128), F32)], axis=0)
        hi = block.astype(BF16)
        lo = (block - hi.astype(F32)).astype(BF16)
        w[k, 0:128, :] = hi
        w[k, 128:256, :] = lo

    def recv_first(d):
        zz = (z + 8 - d) % 8
        if d != 0:
            pltpu.make_async_remote_copy(
                src_ref=comp.at[rows(c, pos)], dst_ref=g.at[zz * 2 + xh, rows(c, pos)],
                send_sem=s1.at[0, d], recv_sem=r1.at[0, d],
                device_id=col[d], device_id_type=MESH).wait_recv()
        pltpu.make_async_remote_copy(
            src_ref=comp.at[rows(c, pos)], dst_ref=g.at[zz * 2 + 1 - xh, rows(c, pos)],
            send_sem=s1.at[1, d], recv_sem=r1.at[1, d],
            device_id=cross[d], device_id_type=MESH).wait_recv()

    later = []
    for i, d in enumerate(ORDER):
        weights(2 * i)
        weights(2 * i + 1)
        if d == 0:
            mine.wait()
        recv_first(d)
        zz = (z + 8 - d) % 8
        part = g.at[pl.ds(zz * 2, 2), rows(c, pos)]
        for j in (2, 1, 3):
            cp = pltpu.make_async_remote_copy(
                src_ref=part, dst_ref=part, send_sem=s2.at[j, d], recv_sem=r2.at[j, d],
                device_id=ring[j], device_id_type=MESH)
            cp.start()
            later.append(cp)
        cp = pltpu.make_async_remote_copy(
            src_ref=part, dst_ref=part, send_sem=s3.at[0, d], recv_sem=r3.at[0, d],
            device_id=twin, device_id_type=MESH)
        cp.start()
        later.append(cp)

    for d in ORDER:
        zz = (z + 8 - d) % 8
        for j in (1, 3, 2):
            part = g.at[pl.ds(zz * 2, 2), rows(c, (pos + 4 - j) % 4)]
            pltpu.make_async_remote_copy(
                src_ref=part, dst_ref=part, send_sem=s2.at[j, d], recv_sem=r2.at[j, d],
                device_id=ring[j], device_id_type=MESH).wait_recv()
            cp = pltpu.make_async_remote_copy(
                src_ref=part, dst_ref=part, send_sem=s3.at[j, d], recv_sem=r3.at[j, d],
                device_id=twin, device_id_type=MESH)
            cp.start()
            later.append(cp)
    other_pos = c * x + (1 - c) * y
    for d in ORDER:
        zz = (z + 8 - d) % 8
        for j in range(4):
            part = g.at[pl.ds(zz * 2, 2), rows(1 - c, (other_pos + 4 - j) % 4)]
            pltpu.make_async_remote_copy(
                src_ref=part, dst_ref=part, send_sem=s3.at[j, d], recv_sem=r3.at[j, d],
                device_id=twin, device_id_type=MESH).wait_recv()
    for cp in first + later:
        cp.wait_send()


def gather(cd, airr, comp, integ):
    smem = pl.BlockSpec(memory_space=pltpu.SMEM)
    vmem = pl.BlockSpec(memory_space=pltpu.VMEM)
    hbm = pl.BlockSpec(memory_space=pl.ANY)
    dma = pltpu.SemaphoreType.DMA
    return pl.pallas_call(
        gather_kernel,
        out_shape=(
            jax.ShapeDtypeStruct((16, SLOTS * 8, 128), F32),
            jax.ShapeDtypeStruct((KT, 256, 128), BF16),
        ),
        in_specs=[smem, smem, vmem, hbm],
        out_specs=(vmem, vmem),
        scratch_shapes=[
            pltpu.VMEM((IRREPS * VB // 8, 8, KT * CD_TILE), F32),
            dma, dma, dma((2, 8)), dma((2, 8)), dma((4, 8)), dma((4, 8)), dma((4, 8)), dma((4, 8)),
        ],
        compiler_params=pltpu.CompilerParams(
            collective_id=0, has_side_effects=True, vmem_limit_bytes=24 * 2**20),
        name="gather",
    )(cd, airr, comp, integ)


def product_kernel(tab, g, w, p, lhs, acc):
    p[ZEROT] = jnp.zeros((8, 128), F32)

    def label(lab, c):
        nr = tab[T_NR + lab]
        nk = tab[T_NK + lab]

        def rowsof(m, c):
            tiles = []
            for t in range(16):
                ok = m * 16 + t < nr
                r = jnp.where(ok, tab[T_LST + lab * TILES + jnp.minimum(m * 16 + t, nr - 1)], 0)
                tiles.append((ok, r, tab[T_OFF + r]))
            acc[...] = jnp.zeros_like(acc)

            def depth(kc, c):
                two = kc * 2 + 1 < nk
                k0 = tab[T_KL + lab * KT + kc * 2]
                k1 = tab[T_KL + lab * KT + jnp.where(two, kc * 2 + 1, kc * 2)]
                for t in range(16):
                    off = tiles[t][2] + kc * 2
                    lhs[t * 8:(t + 1) * 8, 0:128] = g[off]
                    off1 = jnp.where(two, off + 1, off)
                    lhs[t * 8:(t + 1) * 8, 128:256] = jnp.where(two, g[off1], 0.0)
                a = lhs[...]
                hi = a.astype(BF16)
                lo = (a - hi.astype(F32)).astype(BF16)
                ww = jnp.concatenate([w[k0], w[k1]], axis=1)
                nt = (((1,), (1,)), ((), ()))
                big = lax.dot_general(hi, ww, nt, preferred_element_type=F32)
                small = lax.dot_general(lo, ww[:128], nt, preferred_element_type=F32)
                acc[...] += big[:, :128] + (big[:, 128:] + small)
                return c

            lax.fori_loop(0, (nk + 1) // 2, depth, 0)
            for t in range(16):
                ok, r, _ = tiles[t]
                p[jnp.where(ok, r, DUMPT)] = acc[t * 8:(t + 1) * 8, :]
            return c

        return lax.fori_loop(0, (nr + 15) // 16, rowsof, c)

    lax.fori_loop(0, IRREPS, label, 0)


def product(tab, g, w):
    smem = pl.BlockSpec(memory_space=pltpu.SMEM)
    vmem = pl.BlockSpec(memory_space=pltpu.VMEM)
    return pl.pallas_call(
        product_kernel,
        out_shape=jax.ShapeDtypeStruct((PT, 8, 128), F32),
        in_specs=[smem, vmem, vmem],
        out_specs=vmem,
        scratch_shapes=[pltpu.VMEM((128, 256), F32), pltpu.VMEM((128, 128), F32)],
        compiler_params=pltpu.CompilerParams(vmem_limit_bytes=24 * 2**20),
        name="product",
    )(tab, g, w)


def owners_kernel(tab, p, out, send, loc_sem, ss, rs):
    me = lax.axis_index("slab")
    barrier = pltpu.get_barrier_semaphore()
    for i in range(1, 16):
        pl.semaphore_signal(barrier, inc=1, device_id={"slab": (me + i) % 16}, device_id_type=MESH)
    copies = []
    for i in list(range(1, 16)) + [0]:
        o = (me + i) % 16
        block = jnp.concatenate([p[tab[T_SRC + o * CAP + q]] for q in range(CAP)], axis=0)
        send[i] = jnp.transpose(block)[:VP]
        if i == 1:
            pl.semaphore_wait(barrier, 15)
        if i == 0:
            cp = pltpu.make_async_copy(send.at[i], out.at[me], loc_sem)
        else:
            cp = pltpu.make_async_remote_copy(
                src_ref=send.at[i], dst_ref=out.at[me], send_sem=ss.at[i], recv_sem=rs.at[i],
                device_id={"slab": o}, device_id_type=MESH)
        cp.start()
        copies.append(cp)
    for i in range(1, 16):
        src = (me + 16 - i) % 16
        pltpu.make_async_remote_copy(
            src_ref=send.at[i], dst_ref=out.at[src], send_sem=ss.at[i], recv_sem=rs.at[i],
            device_id={"slab": (me + i) % 16}, device_id_type=MESH).wait_recv()
    for cp in copies[:-1]:
        cp.wait_send()
    copies[-1].wait()


def owners(tab, p):
    smem = pl.BlockSpec(memory_space=pltpu.SMEM)
    vmem = pl.BlockSpec(memory_space=pltpu.VMEM)
    dma = pltpu.SemaphoreType.DMA
    return pl.pallas_call(
        owners_kernel,
        out_shape=jax.ShapeDtypeStruct((16, VP, 128), F32),
        in_specs=[smem, vmem],
        out_specs=vmem,
        scratch_shapes=[pltpu.VMEM((16, VP, 128), F32), dma, dma((16,)), dma((16,))],
        compiler_params=pltpu.CompilerParams(
            collective_id=1, has_side_effects=True, vmem_limit_bytes=24 * 2**20),
        name="owners",
    )(tab, p)


def expand_kernel(tab, row, airr, arrived, out):
    s = pl.program_id(0)
    me = lax.axis_index("slab")
    a = airr[s, lax.axis_index("blk")]
    lane = lax.broadcasted_iota(jnp.int32, (1, 128), 1) // 8
    want = jnp.full((1, 128), -1, jnp.int32)
    for q in range(CAP):
        r = tab[T_SRC + me * CAP + q]
        beta = jnp.where(r < TILES, row[jnp.minimum(r, TILES - 1)] ^ a, -1)
        want = jnp.where(lane == q, beta, want)
    block = arrived[0, :VB, :]
    for beta in range(IRREPS):
        out[0, beta * VB:(beta + 1) * VB, :] = jnp.where(want == beta, block, 0.0)


def expand(tab, row, airr, arrived):
    smem = pl.BlockSpec(memory_space=pltpu.SMEM)
    return pl.pallas_call(
        expand_kernel,
        grid=(16,),
        out_shape=jax.ShapeDtypeStruct((16, IRREPS * VB, 128), F32),
        in_specs=[smem, smem, smem, pl.BlockSpec((1, VP, 128), lambda s: (s, 0, 0))],
        out_specs=pl.BlockSpec((1, IRREPS * VB, 128), lambda s: (s, 0, 0)),
        name="expand",
    )(tab, row, airr, arrived)


def dense(amplitude, integ, row, cd, airr, tab):
    slab = lax.axis_index("slab")
    blk = lax.axis_index("blk")
    own_a = airr[slab, blk]
    piece = lax.all_gather(amplitude, "blk", axis=0, tiled=True)
    cd_cols = jnp.repeat(cd, CD_TILE)
    labels = jnp.repeat(row, ROW_TILE)
    coupled = jnp.where(labels[:, None] == cd_cols[None, :], piece, 0.0)
    blocks = integ.reshape(IRREPS, VB, KT * CD_TILE)
    want = cd_cols ^ own_a
    kept = jnp.sum(jnp.where(want[None, None, :] == jnp.arange(IRREPS)[:, None, None], blocks, 0.0), axis=0)
    prod = jnp.dot(coupled, kept.T, precision=lax.Precision.HIGHEST, preferred_element_type=F32)
    prod = jnp.concatenate([prod.reshape(TILES, ROW_TILE, VB), jnp.zeros((1, ROW_TILE, VB), F32)], axis=0)
    packed = jnp.take(prod, tab[T_SRC:T_SRC + 256], axis=0).reshape(16, CAP * ROW_TILE, VB)
    arrived = lax.all_to_all(packed, "slab", split_axis=0, concat_axis=0, tiled=True)
    arrived = jnp.transpose(arrived, (0, 2, 1))
    return jnp.pad(arrived, ((0, 0), (0, VP - VB), (0, 0)))


def shards(amplitude, integrals, row, cd, airr, owner):
    integ = integrals.reshape(KT * CD_TILE, IRREPS * VB).T
    own = owner.reshape(TILES)
    comp, tab = prep(row, cd, own, amplitude)

    def fast(amplitude, integ, row, cd, airr, tab, comp):
        g, w = gather(cd, airr, comp, integ.reshape(IRREPS * VB // 8, 8, KT * CD_TILE))
        p = product(tab, g.reshape(16 * SLOTS, 8, 128), w)
        return owners(tab, p)

    def slow(amplitude, integ, row, cd, airr, tab, comp):
        return dense(amplitude, integ, row, cd, airr, tab)

    arrived = lax.cond(tab[T_FIT] == 1, fast, slow, amplitude, integ, row, cd, airr, tab, comp)
    out = expand(tab, row, airr, arrived)
    return jnp.transpose(out, (2, 0, 1)).reshape(CAP * ROW_TILE, 16, 1, IRREPS * VB)


def solution(mesh):
    return jax.shard_map(
        shards,
        mesh=mesh,
        in_specs=(P("blk", None), P(None, "slab", "blk", None), P(), P(), P(), P()),
        out_specs=P("slab", None, "blk", None),
        check_vma=False,
    )
```

```python
import functools

import jax
import jax.numpy as jnp
from jax import lax
from jax.experimental import pallas as pl
from jax.experimental.pallas import tpu as pltpu
from jax.sharding import PartitionSpec as P

IRREPS = 8
CD_TILE = 128
ROW_TILE = 8
TILES = 128
KT = 16
OWN_TILES = 8
SLOTS = 32
CAP = 16
VB = 100
VP = 104
ZEROT = 128
DUMPT = 129
PT = 136
MT = 24
T_LST = 0
T_KL = 1024
T_SRC = 1152
T_NR = 1408
T_NK = 1416
T_FIT = 1424
T_BETA = 1440
T_A = 1456
T_LAB = 1472
T_NO = 1488
T_SIZE = 1536

MESH = pl.DeviceIdType.MESH
F32 = jnp.float32
BF16 = jnp.bfloat16


def prep_kernel(row, cd, airr, own, amp_hbm, comp, tab, amp, amp_sem):
    slab = lax.axis_index("slab")
    blk = lax.axis_index("blk")
    load = pltpu.make_async_copy(amp_hbm, amp, amp_sem)
    load.start()
    for i in range(IRREPS):
        tab[T_NR + i] = 0
        tab[T_NK + i] = 0
    for i in range(16):
        tab[T_NO + i] = 0
    labs = [cd[k] for k in range(KT)]
    mine = airr[slab, blk]
    for k in range(KT):
        lab = labs[k]
        kap = tab[T_NK + lab]
        tab[T_KL + lab * KT + kap] = k
        tab[T_NK + lab] = kap + 1
        tab[T_BETA + k] = lab ^ mine
    for i in range(16):
        tab[T_A + i] = airr[i, blk]

    def clear(i, c):
        for u in range(32):
            tab[T_SRC + i * 32 + u] = ZEROT
        return c

    lax.fori_loop(0, 8, clear, 0)

    def group(g, most):
        rs = [g * OWN_TILES + t for t in range(OWN_TILES)]
        ls = [row[r] for r in rs]
        os = [own[r] for r in rs]
        ks = [tab[T_NK + lab] for lab in ls]
        acc = g * SLOTS
        for r, lab, o, kn in zip(rs, ls, os, ks):
            p = tab[T_NR + lab]
            q = tab[T_NO + o]
            tab[T_LST + lab * TILES + p] = r + acc * 256
            tab[T_NR + lab] = p + 1
            tab[T_SRC + o * CAP + q] = r
            tab[T_NO + o] = q + 1
            acc = acc + kn
        return jnp.maximum(most, acc - g * SLOTS)

    most = lax.fori_loop(0, TILES // OWN_TILES, group, jnp.int32(0))
    tab[T_FIT] = jnp.where(most <= SLOTS, 1, 0)
    for q in range(CAP):
        tab[T_LAB + q] = row[jnp.minimum(tab[T_SRC + slab * CAP + q], TILES - 1)]

    load.wait()
    j = jnp.int32(0)
    for t in range(OWN_TILES):
        lab = row[blk * OWN_TILES + t]
        for k in range(KT):
            jc = jnp.minimum(j, SLOTS)
            comp[pl.ds(pl.multiple_of(jc * 8, 8), 8), :] = amp[t * 8:(t + 1) * 8, k * 128:(k + 1) * 128]
            j = j + jnp.where(labs[k] == lab, 1, 0)


def prep(row, cd, airr, own, amp):
    smem = pl.BlockSpec(memory_space=pltpu.SMEM)
    vmem = pl.BlockSpec(memory_space=pltpu.VMEM)
    return pl.pallas_call(
        prep_kernel,
        out_shape=(
            jax.ShapeDtypeStruct(((SLOTS + 1) * 8, 128), F32),
            jax.ShapeDtypeStruct((T_SIZE,), jnp.int32),
        ),
        in_specs=[smem, smem, smem, smem, pl.BlockSpec(memory_space=pl.ANY)],
        out_specs=(vmem, smem),
        scratch_shapes=[pltpu.VMEM((OWN_TILES * 8, KT * CD_TILE), F32), pltpu.SemaphoreType.DMA],
        compiler_params=pltpu.CompilerParams(vmem_limit_bytes=50 * 2**20),
        name="prep",
    )(row, cd, airr, own, amp)


ORDER = (0, 1, 7, 2, 6, 3, 5, 4)


def gather_kernel(tab, comp, integ, g, w, raw, loc_sem, raw_sem, s1, r1, s2, r2, s3, r3):
    slab = lax.axis_index("slab")
    blk = lax.axis_index("blk")
    c = slab % 2
    y = (slab // 2) % 4
    xl = slab // 8
    z = blk // 2
    xh = blk % 2
    x = xh * 2 + xl
    pos = (1 - c) * x + c * y

    def dev(x_, y_, z_, c_):
        return {"slab": (x_ % 2) * 8 + y_ * 2 + c_, "blk": z_ * 2 + x_ // 2}

    raw_copy = pltpu.make_async_copy(integ, raw, raw_sem)
    raw_copy.start()

    col = [dev(x, y, (z + d) % 8, c) for d in range(8)]
    cross = [dev(3 - x, y, (z + d) % 8, c) for d in range(8)]
    ring = [None] + [dev((x + (1 - c) * j) % 4, (y + c * j) % 4, z, c) for j in range(1, 4)]
    twin = dev(x, y, z, 1 - c)

    barrier = pltpu.get_barrier_semaphore()
    peers = col[1:] + cross + ring[1:] + [twin]
    for peer in peers:
        pl.semaphore_signal(barrier, inc=1, device_id=peer, device_id_type=MESH)

    def rows(c_, p_):
        return pl.ds(pl.multiple_of(c_ * 128 + p_ * 32, 32), 32)

    mine = pltpu.make_async_copy(comp.at[rows(c, pos)], g.at[blk, rows(c, pos)], loc_sem)
    mine.start()
    pl.semaphore_wait(barrier, len(peers))

    cross_pos = (1 - c) * (3 - x) + c * y
    first = []
    for d in ORDER:
        if d != 0:
            cp = pltpu.make_async_remote_copy(
                src_ref=comp.at[rows(c, pos)], dst_ref=g.at[blk, rows(c, pos)],
                send_sem=s1.at[0, d], recv_sem=r1.at[0, d],
                device_id=col[d], device_id_type=MESH)
            cp.start()
            first.append(cp)
        cp = pltpu.make_async_remote_copy(
            src_ref=comp.at[rows(c, cross_pos)], dst_ref=g.at[blk, rows(c, cross_pos)],
            send_sem=s1.at[1, d], recv_sem=r1.at[1, d],
            device_id=cross[d], device_id_type=MESH)
        cp.start()
        first.append(cp)

    raw_copy.wait()

    def weights(k):
        beta = tab[T_BETA + k]
        odd = beta & 1
        start = beta * 12 + beta // 2
        block = jnp.concatenate([raw[start + i, :, k * 128:(k + 1) * 128] for i in range(VP // 8)], axis=0)
        moved = jnp.concatenate([block[4:], block[:4]], axis=0)
        block = jnp.where(odd == 1, moved, block)
        block = jnp.concatenate([block, jnp.zeros((128 - VP, 128), F32)], axis=0)
        hi = block.astype(BF16)
        lo = (block - hi.astype(F32)).astype(BF16)
        w[k, 0:128, :] = hi
        w[k, 128:256, :] = lo

    def recv_first(d):
        zz = (z + 8 - d) % 8
        if d != 0:
            pltpu.make_async_remote_copy(
                src_ref=comp.at[rows(c, pos)], dst_ref=g.at[zz * 2 + xh, rows(c, pos)],
                send_sem=s1.at[0, d], recv_sem=r1.at[0, d],
                device_id=col[d], device_id_type=MESH).wait_recv()
        pltpu.make_async_remote_copy(
            src_ref=comp.at[rows(c, pos)], dst_ref=g.at[zz * 2 + 1 - xh, rows(c, pos)],
            send_sem=s1.at[1, d], recv_sem=r1.at[1, d],
            device_id=cross[d], device_id_type=MESH).wait_recv()

    later = []
    for i, d in enumerate(ORDER):
        weights(2 * i)
        weights(2 * i + 1)
        if d == 0:
            mine.wait()
        recv_first(d)
        zz = (z + 8 - d) % 8
        part = g.at[pl.ds(zz * 2, 2), rows(c, pos)]
        for j in (2, 1, 3):
            cp = pltpu.make_async_remote_copy(
                src_ref=part, dst_ref=part, send_sem=s2.at[j, d], recv_sem=r2.at[j, d],
                device_id=ring[j], device_id_type=MESH)
            cp.start()
            later.append(cp)
        cp = pltpu.make_async_remote_copy(
            src_ref=part, dst_ref=part, send_sem=s3.at[0, d], recv_sem=r3.at[0, d],
            device_id=twin, device_id_type=MESH)
        cp.start()
        later.append(cp)

    for d in ORDER:
        zz = (z + 8 - d) % 8
        for j in (1, 3, 2):
            part = g.at[pl.ds(zz * 2, 2), rows(c, (pos + 4 - j) % 4)]
            pltpu.make_async_remote_copy(
                src_ref=part, dst_ref=part, send_sem=s2.at[j, d], recv_sem=r2.at[j, d],
                device_id=ring[j], device_id_type=MESH).wait_recv()
            cp = pltpu.make_async_remote_copy(
                src_ref=part, dst_ref=part, send_sem=s3.at[j, d], recv_sem=r3.at[j, d],
                device_id=twin, device_id_type=MESH)
            cp.start()
            later.append(cp)
    other_pos = c * x + (1 - c) * y
    for d in ORDER:
        zz = (z + 8 - d) % 8
        for j in range(4):
            part = g.at[pl.ds(zz * 2, 2), rows(1 - c, (other_pos + 4 - j) % 4)]
            pltpu.make_async_remote_copy(
                src_ref=part, dst_ref=part, send_sem=s3.at[j, d], recv_sem=r3.at[j, d],
                device_id=twin, device_id_type=MESH).wait_recv()
    for cp in first + later:
        cp.wait_send()


def gather(tab, comp, integ):
    smem = pl.BlockSpec(memory_space=pltpu.SMEM)
    vmem = pl.BlockSpec(memory_space=pltpu.VMEM)
    hbm = pl.BlockSpec(memory_space=pl.ANY)
    dma = pltpu.SemaphoreType.DMA
    return pl.pallas_call(
        gather_kernel,
        out_shape=(
            jax.ShapeDtypeStruct((16, SLOTS * 8, 128), F32),
            jax.ShapeDtypeStruct((KT, 256, 128), BF16),
        ),
        in_specs=[smem, vmem, hbm],
        out_specs=(vmem, vmem),
        scratch_shapes=[
            pltpu.VMEM((IRREPS * VB // 8, 8, KT * CD_TILE), F32),
            dma, dma, dma((2, 8)), dma((2, 8)), dma((4, 8)), dma((4, 8)), dma((4, 8)), dma((4, 8)),
        ],
        compiler_params=pltpu.CompilerParams(
            collective_id=0, has_side_effects=True, vmem_limit_bytes=24 * 2**20),
        name="gather",
    )(tab, comp, integ)


def product_kernel(tab, g, w, p, lhs, acc):
    p[ZEROT] = jnp.zeros((8, 128), F32)

    def label(lab, c):
        nr = tab[T_NR + lab]
        nk = tab[T_NK + lab]

        def rowsof(m, c):
            tiles = []
            for t in range(MT):
                ok = m * MT + t < nr
                v = tab[T_LST + lab * TILES + jnp.minimum(m * MT + t, nr - 1)]
                tiles.append((jnp.where(ok, v & 255, DUMPT), v >> 8))
            acc[...] = jnp.zeros_like(acc)

            def depth(kc, c):
                two = kc * 2 + 1 < nk
                k0 = tab[T_KL + lab * KT + kc * 2]
                k1 = tab[T_KL + lab * KT + jnp.where(two, kc * 2 + 1, kc * 2)]
                for t in range(MT):
                    off = tiles[t][1] + kc * 2
                    lhs[t * 8:(t + 1) * 8, 0:128] = g[off]
                    off1 = jnp.where(two, off + 1, off)
                    lhs[t * 8:(t + 1) * 8, 128:256] = jnp.where(two, g[off1], 0.0)
                a = lhs[...]
                hi = a.astype(BF16)
                lo = (a - hi.astype(F32)).astype(BF16)
                ww = jnp.concatenate([w[k0], w[k1]], axis=1)
                nt = (((1,), (1,)), ((), ()))
                big = lax.dot_general(hi, ww, nt, preferred_element_type=F32)
                small = lax.dot_general(lo, ww[:128], nt, preferred_element_type=F32)
                acc[...] += big[:, :128] + (big[:, 128:] + small)
                return c

            lax.fori_loop(0, (nk + 1) // 2, depth, 0)
            for t in range(MT):
                p[tiles[t][0]] = acc[t * 8:(t + 1) * 8, :]
            return c

        return lax.fori_loop(0, (nr + MT - 1) // MT, rowsof, c)

    lax.fori_loop(0, IRREPS, label, 0)


def product(tab, g, w):
    smem = pl.BlockSpec(memory_space=pltpu.SMEM)
    vmem = pl.BlockSpec(memory_space=pltpu.VMEM)
    return pl.pallas_call(
        product_kernel,
        out_shape=jax.ShapeDtypeStruct((PT, 8, 128), F32),
        in_specs=[smem, vmem, vmem],
        out_specs=vmem,
        scratch_shapes=[pltpu.VMEM((MT * 8, 256), F32), pltpu.VMEM((MT * 8, 128), F32)],
        compiler_params=pltpu.CompilerParams(vmem_limit_bytes=24 * 2**20),
        name="product",
    )(tab, g, w)


def owners_kernel(tab, p, out, send, loc_sem, ss, rs):
    me = lax.axis_index("slab")
    barrier = pltpu.get_barrier_semaphore()
    for i in range(1, 16):
        pl.semaphore_signal(barrier, inc=1, device_id={"slab": (me + i) % 16}, device_id_type=MESH)
    copies = []
    for i in list(range(1, 16)) + [0]:
        o = (me + i) % 16
        block = jnp.concatenate([p[tab[T_SRC + o * CAP + q]] for q in range(CAP)], axis=0)
        send[i] = jnp.transpose(block)[:VP]
        if i == 1:
            pl.semaphore_wait(barrier, 15)
        if i == 0:
            cp = pltpu.make_async_copy(send.at[i], out.at[me], loc_sem)
        else:
            cp = pltpu.make_async_remote_copy(
                src_ref=send.at[i], dst_ref=out.at[me], send_sem=ss.at[i], recv_sem=rs.at[i],
                device_id={"slab": o}, device_id_type=MESH)
        cp.start()
        copies.append(cp)
    for i in range(1, 16):
        src = (me + 16 - i) % 16
        pltpu.make_async_remote_copy(
            src_ref=send.at[i], dst_ref=out.at[src], send_sem=ss.at[i], recv_sem=rs.at[i],
            device_id={"slab": (me + i) % 16}, device_id_type=MESH).wait_recv()
    for cp in copies[:-1]:
        cp.wait_send()
    copies[-1].wait()


def owners(tab, p):
    smem = pl.BlockSpec(memory_space=pltpu.SMEM)
    vmem = pl.BlockSpec(memory_space=pltpu.VMEM)
    dma = pltpu.SemaphoreType.DMA
    return pl.pallas_call(
        owners_kernel,
        out_shape=jax.ShapeDtypeStruct((16, VP, 128), F32),
        in_specs=[smem, vmem],
        out_specs=vmem,
        scratch_shapes=[pltpu.VMEM((16, VP, 128), F32), dma, dma((16,)), dma((16,))],
        compiler_params=pltpu.CompilerParams(
            collective_id=1, has_side_effects=True, vmem_limit_bytes=24 * 2**20),
        name="owners",
    )(tab, p)


def expand_kernel(tab, arrived, out, stage, sems):
    lane = lax.broadcasted_iota(jnp.int32, (1, 128), 1) // 8
    lab = jnp.zeros((1, 128), jnp.int32)
    for q in range(CAP):
        lab = jnp.where(lane == q, tab[T_LAB + q], lab)
    upper = lax.broadcasted_iota(jnp.int32, (8, 128), 0) < 4

    def one(s, c):
        want = lab ^ tab[T_A + s]
        block = arrived[s]
        moved = jnp.concatenate([block[100:104], block[0:100]], axis=0)
        for m in range(IRREPS // 2):
            even = want == 2 * m
            odd = want == 2 * m + 1
            base = 2 * VB * m
            stage[s, base:base + 96, :] = jnp.where(even, block[:96], 0.0)
            stage[s, base + 96:base + 104, :] = jnp.where(
                upper, jnp.where(even, block[96:], 0.0), jnp.where(odd, moved[:8], 0.0))
            stage[s, base + 104:base + 200, :] = jnp.where(odd, moved[8:], 0.0)
        pltpu.make_async_copy(stage.at[s], out.at[s], sems.at[s]).start()
        return c

    lax.fori_loop(0, 16, one, 0)
    for s in range(16):
        pltpu.make_async_copy(stage.at[s], out.at[s], sems.at[s]).wait()


def expand(tab, arrived):
    return pl.pallas_call(
        expand_kernel,
        out_shape=jax.ShapeDtypeStruct((16, IRREPS * VB, 128), F32),
        in_specs=[pl.BlockSpec(memory_space=pltpu.SMEM), pl.BlockSpec(memory_space=pltpu.VMEM)],
        out_specs=pl.BlockSpec(memory_space=pl.ANY),
        scratch_shapes=[pltpu.VMEM((16, IRREPS * VB, 128), F32), pltpu.SemaphoreType.DMA((16,))],
        compiler_params=pltpu.CompilerParams(vmem_limit_bytes=40 * 2**20),
        name="expand",
    )(tab, arrived)


def dense(amplitude, integ, row, cd, airr, tab):
    slab = lax.axis_index("slab")
    blk = lax.axis_index("blk")
    own_a = airr[slab, blk]
    copies = jnp.broadcast_to(amplitude[None], (16,) + amplitude.shape)
    piece = lax.all_to_all(copies, "blk", split_axis=0, concat_axis=0, tiled=True).reshape(-1, KT * CD_TILE)
    cd_cols = jnp.repeat(cd, CD_TILE)
    labels = jnp.repeat(row, ROW_TILE)
    coupled = jnp.where(labels[:, None] == cd_cols[None, :], piece, 0.0)
    blocks = integ.reshape(IRREPS, VB, KT * CD_TILE)
    want = cd_cols ^ own_a
    kept = jnp.sum(jnp.where(want[None, None, :] == jnp.arange(IRREPS)[:, None, None], blocks, 0.0), axis=0)
    prod = jnp.dot(coupled, kept.T, precision=lax.Precision.HIGHEST, preferred_element_type=F32)
    prod = jnp.concatenate([prod.reshape(TILES, ROW_TILE, VB), jnp.zeros((1, ROW_TILE, VB), F32)], axis=0)
    packed = jnp.take(prod, tab[T_SRC:T_SRC + 256], axis=0).reshape(16, CAP * ROW_TILE, VB)
    arrived = lax.all_to_all(packed, "slab", split_axis=0, concat_axis=0, tiled=True)
    arrived = jnp.transpose(arrived, (0, 2, 1))
    return jnp.pad(arrived, ((0, 0), (0, VP - VB), (0, 0)))


def shards(amplitude, integrals, row, cd, airr, owner):
    integ = integrals.reshape(KT * CD_TILE, IRREPS * VB).T
    own = owner.reshape(TILES)
    comp, tab = prep(row, cd, airr, own, amplitude)

    def fast(amplitude, integ, row, cd, airr, tab, comp):
        g, w = gather(tab, comp, integ.reshape(IRREPS * VB // 8, 8, KT * CD_TILE))
        p = product(tab, g.reshape(16 * SLOTS, 8, 128), w)
        return owners(tab, p)

    def slow(amplitude, integ, row, cd, airr, tab, comp):
        return dense(amplitude, integ, row, cd, airr, tab)

    arrived = lax.cond(tab[T_FIT] == 1, fast, slow, amplitude, integ, row, cd, airr, tab, comp)
    out = expand(tab, arrived)
    return jnp.transpose(out, (2, 0, 1)).reshape(CAP * ROW_TILE, 16, 1, IRREPS * VB)


def solution(mesh):
    return jax.shard_map(
        shards,
        mesh=mesh,
        in_specs=(P("blk", None), P(None, "slab", "blk", None), P(), P(), P(), P()),
        out_specs=P("slab", None, "blk", None),
        check_vma=False,
    )
```

```python
import functools

import jax
import jax.numpy as jnp
from jax import lax
from jax.experimental import pallas as pl
from jax.experimental.pallas import tpu as pltpu
from jax.sharding import PartitionSpec as P

IRREPS = 8
CD_TILE = 128
ROW_TILE = 8
TILES = 128
KT = 16
OWN_TILES = 8
SLOTS = 32
CAP = 16
VB = 100
VP = 104
ZEROT = 128
DUMPT = 129
PT = 136
MT = 24
KC = 2
T_LST = 0
T_SRC = 1
T_START = 3
T_KL = 4
T_NK = 5
T_LAB = 6

MESH = pl.DeviceIdType.MESH
F32 = jnp.float32
BF16 = jnp.bfloat16


ORDER = (0, 2, 6, 1, 7, 3, 5, 4)


def gather_kernel(row, cd, airr, row_v, own_v, amp_hbm, integ, g, w, tab, fit, comp, found, found_s, raw, amp, amp_sem, found_sem, loc_sem, raw_sem, s1, r1, s2, r2, s3, r3):
    slab = lax.axis_index("slab")
    blk = lax.axis_index("blk")
    c = slab % 2
    y = (slab // 2) % 4
    xl = slab // 8
    z = blk // 2
    xh = blk % 2
    x = xh * 2 + xl
    pos = (1 - c) * x + c * y

    def dev(x_, y_, z_, c_):
        return {"slab": (x_ % 2) * 8 + y_ * 2 + c_, "blk": z_ * 2 + x_ // 2}

    amp_copy = pltpu.make_async_copy(amp_hbm, amp, amp_sem)
    amp_copy.start()
    raw_copy = pltpu.make_async_copy(integ, raw, raw_sem)
    raw_copy.start()

    near = {d: dev(x, y, (z + d) % 8, c) for d in (1, 7, 2, 6)}
    cross = {d: dev(3 - x, y, (z + d) % 8, c) for d in (0, 1, 7, 2, 6)}
    ring = [None] + [dev((x + (1 - c) * j) % 4, (y + c * j) % 4, z, c) for j in range(1, 4)]
    twin = dev(x, y, z, 1 - c)

    barrier = pltpu.get_barrier_semaphore()
    peers = list(near.values()) + list(cross.values()) + ring[1:] + [twin]
    for peer in peers:
        pl.semaphore_signal(barrier, inc=1, device_id=peer, device_id_type=MESH)

    def rows(c_, p_):
        return pl.ds(pl.multiple_of(c_ * 128 + p_ * 32, 32), 32)

    labs = [cd[k] for k in range(KT)]
    sub = lax.broadcasted_iota(jnp.int32, (128, 128), 0)
    lane = lax.broadcasted_iota(jnp.int32, (128, 128), 1)
    one_lane = lax.broadcasted_iota(jnp.int32, (1, 128), 1)

    def coupled_at(place):
        left = jnp.zeros(place.shape, jnp.int32)
        for t in range(OWN_TILES):
            left = jnp.where(place // KT == t, row[blk * OWN_TILES + t], left)
        right = jnp.zeros(place.shape, jnp.int32)
        for k in range(KT):
            right = jnp.where(place % KT == k, labs[k], right)
        return left == right

    down = coupled_at(lax.broadcasted_iota(jnp.int32, (128, 1), 0))
    across = jnp.where(coupled_at(one_lane), 1, 0)
    ahead = jnp.sum(jnp.where(lane < sub, across, 0), axis=1, keepdims=True)
    place = jnp.where(down, ahead, -1)
    found[...] = jnp.sum(jnp.where(place == lane, sub, 0), axis=0, keepdims=True)
    move = pltpu.make_async_copy(found, found_s, found_sem)
    move.start()
    move.wait()
    amp_copy.wait()
    for j in range(SLOTS):
        comp[j * 8:(j + 1) * 8, :] = amp[found_s[0, j]]

    mine = pltpu.make_async_copy(comp.at[rows(c, pos)], g.at[blk, rows(c, pos)], loc_sem)
    mine.start()
    pl.semaphore_wait(barrier, len(peers))

    cross_pos = (1 - c) * (3 - x) + c * y
    first = []
    for d in (2, 6, 0, 1, 7):
        if d != 0:
            cp = pltpu.make_async_remote_copy(
                src_ref=comp.at[rows(c, pos)], dst_ref=g.at[blk, rows(c, pos)],
                send_sem=s1.at[0, d], recv_sem=r1.at[0, d],
                device_id=near[d], device_id_type=MESH)
            cp.start()
            first.append(cp)
        cp = pltpu.make_async_remote_copy(
            src_ref=comp.at[rows(c, cross_pos)], dst_ref=g.at[blk, rows(c, cross_pos)],
            send_sem=s1.at[1, d], recv_sem=r1.at[1, d],
            device_id=cross[d], device_id_type=MESH)
        cp.start()
        first.append(cp)

    row_l = row_v[...]
    own_l = own_v[...]
    diag = sub == lane
    row_c = jnp.sum(jnp.where(diag, row_l, 0), axis=1, keepdims=True)
    own_c = jnp.sum(jnp.where(diag, own_l, 0), axis=1, keepdims=True)
    before = lane < sub
    sub_c = lax.broadcasted_iota(jnp.int32, (128, 1), 0)
    rank = jnp.sum(jnp.where((own_l == own_c) & before, 1, 0), axis=1, keepdims=True)
    target = own_c * CAP + rank
    for h in range(2):
        tab[T_SRC + h:T_SRC + h + 1, :] = ZEROT + jnp.sum(
            jnp.where(target == lane + h * 128, sub - ZEROT, 0), axis=0, keepdims=True)
    tab[T_LAB:T_LAB + 1, :] = jnp.sum(
        jnp.where(target == slab * CAP + lane // ROW_TILE, row_c, 0), axis=0, keepdims=True)
    order = jnp.sum(jnp.where((row_l < row_c) | ((row_l == row_c) & before), 1, 0), axis=1, keepdims=True)
    nk_l = jnp.zeros((1, 128), jnp.int32)
    nk_c = jnp.zeros((128, 1), jnp.int32)
    nk_of = jnp.zeros((1, 128), jnp.int32)
    list_l = jnp.zeros((1, 128), jnp.int32)
    for k in range(KT):
        nk_l = nk_l + jnp.where(row_l == labs[k], 1, 0)
        nk_c = nk_c + jnp.where(row_c == labs[k], 1, 0)
        nk_of = nk_of + jnp.where(one_lane == labs[k], 1, 0)
        kap = jnp.int32(0)
        for other in range(k):
            kap = kap + jnp.where(labs[other] == labs[k], 1, 0)
        list_l = list_l + jnp.where(one_lane == labs[k] * KT + kap, k, 0)
    same = (lane // OWN_TILES == sub // OWN_TILES) & before
    inside = jnp.sum(jnp.where(same, nk_l, 0), axis=1, keepdims=True)
    value = sub_c + 256 * (SLOTS * (sub_c // OWN_TILES) + inside)
    tab[T_LST:T_LST + 1, :] = jnp.sum(jnp.where(order == lane, value, 0), axis=0, keepdims=True)
    tab[T_START:T_START + 1, :] = jnp.sum(jnp.where(row_c < lane, 1, 0), axis=0, keepdims=True)
    tab[T_KL:T_KL + 1, :] = list_l
    tab[T_NK:T_NK + 1, :] = nk_of
    tab[7:8, :] = jnp.zeros((1, 128), jnp.int32)
    fit[0] = jnp.where(jnp.max(inside + nk_c) <= SLOTS, 1, 0)

    raw_copy.wait()
    own_a = airr[slab, blk]

    def weights(k):
        beta = labs[k] ^ own_a
        odd = beta & 1
        start = beta * 12 + beta // 2
        block = jnp.concatenate([raw[start + i, :, k * 128:(k + 1) * 128] for i in range(VP // 8)], axis=0)
        moved = jnp.concatenate([block[4:], block[:4]], axis=0)
        block = jnp.where(odd == 1, moved, block)
        block = jnp.concatenate([block, jnp.zeros((128 - VP, 128), F32)], axis=0)
        hi = block.astype(BF16)
        lo = (block - hi.astype(F32)).astype(BF16)
        w[k, 0:128, :] = hi
        w[k, 128:256, :] = lo

    def plane(d):
        return (z + 8 - d) % 8

    def piece(d, e):
        return g.at[plane(d) * 2 + (xh if e == 0 else 1 - xh), rows(c, pos)]

    def both(d):
        return g.at[pl.ds(plane(d) * 2, 2), rows(c, pos)]

    def recv_first(d):
        for e in ((1,) if d == 0 else (0, 1)):
            pltpu.make_async_remote_copy(
                src_ref=piece(d, e), dst_ref=piece(d, e), send_sem=s1.at[e, d], recv_sem=r1.at[e, d],
                device_id=twin, device_id_type=MESH).wait_recv()

    def relay(ref, d, e, device, start):
        cp = pltpu.make_async_remote_copy(
            src_ref=ref, dst_ref=ref, send_sem=s1.at[e, d], recv_sem=r1.at[e, d],
            device_id=device, device_id_type=MESH)
        if start:
            cp.start()
            later.append(cp)
        else:
            cp.wait_recv()

    def relayed(d):
        if d == 4:
            relay(piece(4, 0), 4, 0, near[2], False)
            relay(piece(4, 1), 4, 1, near[6], False)
        else:
            relay(both(d), d, 0, near[1 if d == 3 else 7], False)

    later = []
    for i, d in enumerate(ORDER):
        weights(2 * i)
        weights(2 * i + 1)
        if d == 0:
            mine.wait()
        if d in (3, 4, 5):
            relayed(d)
        else:
            recv_first(d)
        if d == 2:
            relay(both(2), 3, 0, near[1], True)
            relay(piece(2, 0), 4, 0, near[2], True)
        if d == 6:
            relay(both(6), 5, 0, near[7], True)
            relay(piece(6, 1), 4, 1, near[6], True)
        zz = plane(d)
        part = g.at[pl.ds(zz * 2, 2), rows(c, pos)]
        for j in (2, 1, 3):
            cp = pltpu.make_async_remote_copy(
                src_ref=part, dst_ref=part, send_sem=s2.at[j, d], recv_sem=r2.at[j, d],
                device_id=ring[j], device_id_type=MESH)
            cp.start()
            later.append(cp)
        cp = pltpu.make_async_remote_copy(
            src_ref=part, dst_ref=part, send_sem=s3.at[0, d], recv_sem=r3.at[0, d],
            device_id=twin, device_id_type=MESH)
        cp.start()
        later.append(cp)

    for d in ORDER:
        zz = (z + 8 - d) % 8
        for j in (1, 3, 2):
            part = g.at[pl.ds(zz * 2, 2), rows(c, (pos + 4 - j) % 4)]
            pltpu.make_async_remote_copy(
                src_ref=part, dst_ref=part, send_sem=s2.at[j, d], recv_sem=r2.at[j, d],
                device_id=ring[j], device_id_type=MESH).wait_recv()
            cp = pltpu.make_async_remote_copy(
                src_ref=part, dst_ref=part, send_sem=s3.at[j, d], recv_sem=r3.at[j, d],
                device_id=twin, device_id_type=MESH)
            cp.start()
            later.append(cp)
    other_pos = c * x + (1 - c) * y
    for d in ORDER:
        zz = (z + 8 - d) % 8
        for j in range(4):
            part = g.at[pl.ds(zz * 2, 2), rows(1 - c, (other_pos + 4 - j) % 4)]
            pltpu.make_async_remote_copy(
                src_ref=part, dst_ref=part, send_sem=s3.at[j, d], recv_sem=r3.at[j, d],
                device_id=twin, device_id_type=MESH).wait_recv()
    for cp in first + later:
        cp.wait_send()


def gather(row, cd, airr, own, amp, integ):
    smem = pl.BlockSpec(memory_space=pltpu.SMEM)
    vmem = pl.BlockSpec(memory_space=pltpu.VMEM)
    hbm = pl.BlockSpec(memory_space=pl.ANY)
    dma = pltpu.SemaphoreType.DMA
    return pl.pallas_call(
        gather_kernel,
        out_shape=(
            jax.ShapeDtypeStruct((16, SLOTS * 8, 128), F32),
            jax.ShapeDtypeStruct((KT, 256, 128), BF16),
            jax.ShapeDtypeStruct((8, 128), jnp.int32),
            jax.ShapeDtypeStruct((1,), jnp.int32),
        ),
        in_specs=[smem, smem, smem, vmem, vmem, hbm, hbm],
        out_specs=(vmem, vmem, vmem, smem),
        scratch_shapes=[
            pltpu.VMEM((SLOTS * 8, 128), F32),
            pltpu.VMEM((1, 128), jnp.int32),
            pltpu.SMEM((1, 128), jnp.int32),
            pltpu.VMEM((IRREPS * VB // 8, 8, KT * CD_TILE), F32),
            pltpu.VMEM((OWN_TILES * KT, ROW_TILE, CD_TILE), F32),
            dma, dma, dma, dma, dma((2, 8)), dma((2, 8)), dma((4, 8)), dma((4, 8)), dma((4, 8)), dma((4, 8)),
        ],
        compiler_params=pltpu.CompilerParams(
            collective_id=0, has_side_effects=True, vmem_limit_bytes=24 * 2**20),
        name="gather",
    )(row, cd, airr, row.reshape(1, TILES), own, amp, integ)


def product_kernel(tab, g, w, p, lhs, acc):
    p[ZEROT] = jnp.zeros((8, 128), F32)

    def label(lab, c):
        first = tab[T_START, lab]
        nr = tab[T_START, lab + 1] - first
        nk = tab[T_NK, lab]

        def rowsof(m, c):
            tiles = []
            for t in range(MT):
                ok = m * MT + t < nr
                v = tab[T_LST, first + jnp.minimum(m * MT + t, nr - 1)]
                tiles.append((jnp.where(ok, v & 255, DUMPT), v >> 8))
            acc[...] = jnp.zeros_like(acc)

            def depth(kc, c):
                ks = [kc * KC + h for h in range(KC)]
                have = [k < nk for k in ks]
                cols = [tab[T_KL, lab * KT + jnp.where(ok, k, 0)] for ok, k in zip(have, ks)]
                for t in range(MT):
                    off = tiles[t][1]
                    for h in range(KC):
                        src = g[jnp.minimum(off + jnp.where(have[h], ks[h], 0), 16 * SLOTS - 1)]
                        if h > 0:
                            src = jnp.where(have[h], src, 0.0)
                        lhs[t * 8:(t + 1) * 8, h * 128:(h + 1) * 128] = src
                a = lhs[...]
                hi = a.astype(BF16)
                lo = (a - hi.astype(F32)).astype(BF16)
                ww = jnp.concatenate([w[k] for k in cols], axis=1)
                nt = (((1,), (1,)), ((), ()))
                big = lax.dot_general(hi, ww, nt, preferred_element_type=F32)
                small = lax.dot_general(lo, ww[:128], nt, preferred_element_type=F32)
                acc[...] += big[:, :128] + (big[:, 128:] + small)
                return c

            lax.fori_loop(0, (nk + KC - 1) // KC, depth, 0)
            for t in range(MT):
                p[tiles[t][0]] = acc[t * 8:(t + 1) * 8, :]
            return c

        return lax.fori_loop(0, (nr + MT - 1) // MT, rowsof, c)

    lax.fori_loop(0, IRREPS, label, 0)


def product(tab, g, w):
    smem = pl.BlockSpec(memory_space=pltpu.SMEM)
    vmem = pl.BlockSpec(memory_space=pltpu.VMEM)
    return pl.pallas_call(
        product_kernel,
        out_shape=jax.ShapeDtypeStruct((PT, 8, 128), F32),
        in_specs=[smem, vmem, vmem],
        out_specs=vmem,
        scratch_shapes=[pltpu.VMEM((MT * 8, KC * 128), F32), pltpu.VMEM((MT * 8, 128), F32)],
        compiler_params=pltpu.CompilerParams(vmem_limit_bytes=24 * 2**20),
        name="product",
    )(tab, g, w)


def owners_kernel(tab, p, out, send, loc_sem, ss, rs):
    me = lax.axis_index("slab")
    barrier = pltpu.get_barrier_semaphore()
    for i in range(1, 16):
        pl.semaphore_signal(barrier, inc=1, device_id={"slab": (me + i) % 16}, device_id_type=MESH)
    copies = []
    for i in list(range(1, 16)) + [0]:
        o = (me + i) % 16
        block = jnp.concatenate([p[tab[T_SRC + o // 8, o % 8 * CAP + q]] for q in range(CAP)], axis=0)
        send[i] = jnp.transpose(block)[:VP]
        if i == 1:
            pl.semaphore_wait(barrier, 15)
        if i == 0:
            cp = pltpu.make_async_copy(send.at[i], out.at[me], loc_sem)
        else:
            cp = pltpu.make_async_remote_copy(
                src_ref=send.at[i], dst_ref=out.at[me], send_sem=ss.at[i], recv_sem=rs.at[i],
                device_id={"slab": o}, device_id_type=MESH)
        cp.start()
        copies.append(cp)
    for i in range(1, 16):
        src = (me + 16 - i) % 16
        pltpu.make_async_remote_copy(
            src_ref=send.at[i], dst_ref=out.at[src], send_sem=ss.at[i], recv_sem=rs.at[i],
            device_id={"slab": (me + i) % 16}, device_id_type=MESH).wait_recv()
    for cp in copies[:-1]:
        cp.wait_send()
    copies[-1].wait()


def owners(tab, p):
    smem = pl.BlockSpec(memory_space=pltpu.SMEM)
    vmem = pl.BlockSpec(memory_space=pltpu.VMEM)
    dma = pltpu.SemaphoreType.DMA
    return pl.pallas_call(
        owners_kernel,
        out_shape=jax.ShapeDtypeStruct((16, VP, 128), F32),
        in_specs=[smem, vmem],
        out_specs=vmem,
        scratch_shapes=[pltpu.VMEM((16, VP, 128), F32), dma, dma((16,)), dma((16,))],
        compiler_params=pltpu.CompilerParams(
            collective_id=1, has_side_effects=True, vmem_limit_bytes=24 * 2**20),
        name="owners",
    )(tab, p)


def expand_kernel(airr, tab, arrived, out, stage, sems):
    blk = lax.axis_index("blk")
    lab = tab[T_LAB:T_LAB + 1, :]
    upper = lax.broadcasted_iota(jnp.int32, (8, 128), 0) < 4

    def one(s, c):
        want = lab ^ airr[s, blk]
        block = arrived[s]
        moved = jnp.concatenate([block[100:104], block[0:100]], axis=0)
        for m in range(IRREPS // 2):
            even = want == 2 * m
            odd = want == 2 * m + 1
            base = 2 * VB * m
            stage[s, base:base + 96, :] = jnp.where(even, block[:96], 0.0)
            stage[s, base + 96:base + 104, :] = jnp.where(
                upper, jnp.where(even, block[96:], 0.0), jnp.where(odd, moved[:8], 0.0))
            stage[s, base + 104:base + 200, :] = jnp.where(odd, moved[8:], 0.0)
        pltpu.make_async_copy(stage.at[s], out.at[s], sems.at[s]).start()
        return c

    lax.fori_loop(0, 16, one, 0)
    for s in range(16):
        pltpu.make_async_copy(stage.at[s], out.at[s], sems.at[s]).wait()


def expand(airr, tab, arrived):
    return pl.pallas_call(
        expand_kernel,
        out_shape=jax.ShapeDtypeStruct((16, IRREPS * VB, 128), F32),
        in_specs=[pl.BlockSpec(memory_space=pltpu.SMEM)] + [pl.BlockSpec(memory_space=pltpu.VMEM)] * 2,
        out_specs=pl.BlockSpec(memory_space=pl.ANY),
        scratch_shapes=[pltpu.VMEM((16, IRREPS * VB, 128), F32), pltpu.SemaphoreType.DMA((16,))],
        compiler_params=pltpu.CompilerParams(vmem_limit_bytes=40 * 2**20),
        name="expand",
    )(airr, tab, arrived)


def dense(amplitude, integ, row, cd, airr, tab):
    slab = lax.axis_index("slab")
    blk = lax.axis_index("blk")
    own_a = airr[slab, blk]
    copies = jnp.broadcast_to(amplitude[None], (16,) + amplitude.shape)
    piece = lax.all_to_all(copies, "blk", split_axis=0, concat_axis=0, tiled=True).reshape(-1, KT * CD_TILE)
    cd_cols = jnp.repeat(cd, CD_TILE)
    labels = jnp.repeat(row, ROW_TILE)
    coupled = jnp.where(labels[:, None] == cd_cols[None, :], piece, 0.0)
    blocks = integ.reshape(IRREPS, VB, KT * CD_TILE)
    want = cd_cols ^ own_a
    kept = jnp.sum(jnp.where(want[None, None, :] == jnp.arange(IRREPS)[:, None, None], blocks, 0.0), axis=0)
    prod = jnp.dot(coupled, kept.T, precision=lax.Precision.HIGHEST, preferred_element_type=F32)
    prod = jnp.concatenate([prod.reshape(TILES, ROW_TILE, VB), jnp.zeros((1, ROW_TILE, VB), F32)], axis=0)
    packed = jnp.take(prod, tab[T_SRC:T_SRC + 2].reshape(-1), axis=0).reshape(16, CAP * ROW_TILE, VB)
    arrived = lax.all_to_all(packed, "slab", split_axis=0, concat_axis=0, tiled=True)
    arrived = jnp.transpose(arrived, (0, 2, 1))
    return jnp.pad(arrived, ((0, 0), (0, VP - VB), (0, 0)))


def shards(amplitude, integrals, row, cd, airr, owner):
    integ = integrals.reshape(KT * CD_TILE, IRREPS * VB).T
    amp = amplitude.reshape(OWN_TILES, ROW_TILE, KT, CD_TILE).transpose(0, 2, 1, 3)
    g, w, tab, fit = gather(
        row, cd, airr, owner.reshape(1, TILES), amp.reshape(OWN_TILES * KT, ROW_TILE, CD_TILE),
        integ.reshape(IRREPS * VB // 8, 8, KT * CD_TILE))

    p = product(tab, g.reshape(16 * SLOTS, 8, 128), w)

    def fast(amplitude, integ, row, cd, airr, tab, p):
        return owners(tab, p)

    def slow(amplitude, integ, row, cd, airr, tab, p):
        return dense(amplitude, integ, row, cd, airr, tab)

    arrived = lax.cond(fit[0] == 1, fast, slow, amplitude, integ, row, cd, airr, tab, p)
    out = expand(airr, tab, arrived)
    return jnp.transpose(out, (2, 0, 1)).reshape(CAP * ROW_TILE, 16, 1, IRREPS * VB)


def solution(mesh):
    return jax.shard_map(
        shards,
        mesh=mesh,
        in_specs=(P("blk", None), P(None, "slab", "blk", None), P(), P(), P(), P()),
        out_specs=P("slab", None, "blk", None),
        check_vma=False,
    )
```

```python
import functools

import jax
import jax.numpy as jnp
from jax import lax
from jax.experimental import pallas as pl
from jax.experimental.pallas import tpu as pltpu
from jax.sharding import PartitionSpec as P

IRREPS = 8
CD_TILE = 128
ROW_TILE = 8
TILES = 128
KT = 16
OWN_TILES = 8
SLOTS = 32
CAP = 16
VB = 100
VP = 104
ZEROT = 128
DUMPT = 129
PT = 136
SENT = 100
MT = 24
KC = 2
T_LST = 0
T_SRC = 1
T_START = 3
T_KL = 4
T_NK = 5
T_LAB = 6

MESH = pl.DeviceIdType.MESH
F32 = jnp.float32
BF16 = jnp.bfloat16


ORDER = (0, 2, 6, 1, 7, 3, 5, 4)


def gather_kernel(row, cd, airr, row_v, own_v, amp_hbm, integ, g, w, tab, fit, comp, found, found_s, raw, amp, amp_sem, found_sem, loc_sem, raw_sem, s1, r1, s2, r2, s3, r3):
    slab = lax.axis_index("slab")
    blk = lax.axis_index("blk")
    c = slab % 2
    y = (slab // 2) % 4
    xl = slab // 8
    z = blk // 2
    xh = blk % 2
    x = xh * 2 + xl
    pos = (1 - c) * x + c * y

    def dev(x_, y_, z_, c_):
        return {"slab": (x_ % 2) * 8 + y_ * 2 + c_, "blk": z_ * 2 + x_ // 2}

    amp_copy = pltpu.make_async_copy(amp_hbm, amp, amp_sem)
    amp_copy.start()
    raw_copy = pltpu.make_async_copy(integ, raw, raw_sem)
    raw_copy.start()

    near = {d: dev(x, y, (z + d) % 8, c) for d in (1, 7, 2, 6)}
    cross = {d: dev(3 - x, y, (z + d) % 8, c) for d in (0, 1, 7, 2, 6)}
    ring = [None] + [dev((x + (1 - c) * j) % 4, (y + c * j) % 4, z, c) for j in range(1, 4)]
    twin = dev(x, y, z, 1 - c)

    barrier = pltpu.get_barrier_semaphore()
    peers = list(near.values()) + list(cross.values()) + ring[1:] + [twin]
    for peer in peers:
        pl.semaphore_signal(barrier, inc=1, device_id=peer, device_id_type=MESH)

    def rows(c_, p_):
        return pl.ds(pl.multiple_of(c_ * 128 + p_ * 32, 32), 32)

    labs = [cd[k] for k in range(KT)]
    sub = lax.broadcasted_iota(jnp.int32, (128, 128), 0)
    lane = lax.broadcasted_iota(jnp.int32, (128, 128), 1)
    one_lane = lax.broadcasted_iota(jnp.int32, (1, 128), 1)

    def coupled_at(place):
        left = jnp.zeros(place.shape, jnp.int32)
        for t in range(OWN_TILES):
            left = jnp.where(place // KT == t, row[blk * OWN_TILES + t], left)
        right = jnp.zeros(place.shape, jnp.int32)
        for k in range(KT):
            right = jnp.where(place % KT == k, labs[k], right)
        return left == right

    down = coupled_at(lax.broadcasted_iota(jnp.int32, (128, 1), 0))
    across = jnp.where(coupled_at(one_lane), 1, 0)
    ahead = jnp.sum(jnp.where(lane < sub, across, 0), axis=1, keepdims=True)
    place = jnp.where(down, ahead, -1)
    found[...] = jnp.sum(jnp.where(place == lane, sub, 0), axis=0, keepdims=True)
    move = pltpu.make_async_copy(found, found_s, found_sem)
    move.start()
    move.wait()
    amp_copy.wait()
    for j in range(SLOTS):
        comp[j * 8:(j + 1) * 8, :] = amp[found_s[0, j]]

    mine = pltpu.make_async_copy(comp.at[rows(c, pos)], g.at[blk, rows(c, pos)], loc_sem)
    mine.start()
    pl.semaphore_wait(barrier, len(peers))

    cross_pos = (1 - c) * (3 - x) + c * y
    first = []
    for d in (2, 6, 0, 1, 7):
        if d != 0:
            cp = pltpu.make_async_remote_copy(
                src_ref=comp.at[rows(c, pos)], dst_ref=g.at[blk, rows(c, pos)],
                send_sem=s1.at[0, d], recv_sem=r1.at[0, d],
                device_id=near[d], device_id_type=MESH)
            cp.start()
            first.append(cp)
        cp = pltpu.make_async_remote_copy(
            src_ref=comp.at[rows(c, cross_pos)], dst_ref=g.at[blk, rows(c, cross_pos)],
            send_sem=s1.at[1, d], recv_sem=r1.at[1, d],
            device_id=cross[d], device_id_type=MESH)
        cp.start()
        first.append(cp)

    raw_copy.wait()
    own_a = airr[slab, blk]

    def tables():
        row_l = row_v[...]
        own_l = own_v[...]
        diag = sub == lane
        row_c = jnp.sum(jnp.where(diag, row_l, 0), axis=1, keepdims=True)
        own_c = jnp.sum(jnp.where(diag, own_l, 0), axis=1, keepdims=True)
        before = lane < sub
        sub_c = lax.broadcasted_iota(jnp.int32, (128, 1), 0)
        rank = jnp.sum(jnp.where((own_l == own_c) & before, 1, 0), axis=1, keepdims=True)
        target = own_c * CAP + rank
        for h in range(2):
            tab[T_SRC + h:T_SRC + h + 1, :] = ZEROT + jnp.sum(
                jnp.where(target == lane + h * 128, sub - ZEROT, 0), axis=0, keepdims=True)
        tab[T_LAB:T_LAB + 1, :] = jnp.sum(
            jnp.where(target == slab * CAP + lane // ROW_TILE, row_c, 0), axis=0, keepdims=True)
        order = jnp.sum(jnp.where((row_l < row_c) | ((row_l == row_c) & before), 1, 0), axis=1, keepdims=True)
        nk_l = jnp.zeros((1, 128), jnp.int32)
        nk_c = jnp.zeros((128, 1), jnp.int32)
        nk_of = jnp.zeros((1, 128), jnp.int32)
        list_l = jnp.zeros((1, 128), jnp.int32)
        for k in range(KT):
            nk_l = nk_l + jnp.where(row_l == labs[k], 1, 0)
            nk_c = nk_c + jnp.where(row_c == labs[k], 1, 0)
            nk_of = nk_of + jnp.where(one_lane == labs[k], 1, 0)
            kap = jnp.int32(0)
            for other in range(k):
                kap = kap + jnp.where(labs[other] == labs[k], 1, 0)
            list_l = list_l + jnp.where(one_lane == labs[k] * KT + kap, k, 0)
        same = (lane // OWN_TILES == sub // OWN_TILES) & before
        inside = jnp.sum(jnp.where(same, nk_l, 0), axis=1, keepdims=True)
        value = sub_c + 256 * (SLOTS * (sub_c // OWN_TILES) + inside)
        tab[T_LST:T_LST + 1, :] = jnp.sum(jnp.where(order == lane, value, 0), axis=0, keepdims=True)
        tab[T_START:T_START + 1, :] = jnp.sum(jnp.where(row_c < lane, 1, 0), axis=0, keepdims=True)
        tab[T_KL:T_KL + 1, :] = list_l
        tab[T_NK:T_NK + 1, :] = nk_of
        tab[7:8, :] = jnp.zeros((1, 128), jnp.int32)
        fit[0] = jnp.where(jnp.max(inside + nk_c) <= SLOTS, 1, 0)

    def weights(k):
        beta = labs[k] ^ own_a
        odd = beta & 1
        start = beta * 12 + beta // 2
        block = jnp.concatenate([raw[start + i, :, k * 128:(k + 1) * 128] for i in range(VP // 8)], axis=0)
        moved = jnp.concatenate([block[4:], block[:4]], axis=0)
        block = jnp.where(odd == 1, moved, block)
        block = jnp.concatenate([block, jnp.zeros((128 - VP, 128), F32)], axis=0)
        block = jnp.transpose(block)
        hi = block.astype(BF16)
        lo = (block - hi.astype(F32)).astype(BF16)
        w[k, :, 0:128] = hi
        w[k, :, 128:256] = lo

    def plane(d):
        return (z + 8 - d) % 8

    def piece(d, e):
        return g.at[plane(d) * 2 + (xh if e == 0 else 1 - xh), rows(c, pos)]

    def both(d):
        return g.at[pl.ds(plane(d) * 2, 2), rows(c, pos)]

    def recv_first(d):
        for e in ((1,) if d == 0 else (0, 1)):
            pltpu.make_async_remote_copy(
                src_ref=piece(d, e), dst_ref=piece(d, e), send_sem=s1.at[e, d], recv_sem=r1.at[e, d],
                device_id=twin, device_id_type=MESH).wait_recv()

    def relay(ref, d, e, device, start):
        cp = pltpu.make_async_remote_copy(
            src_ref=ref, dst_ref=ref, send_sem=s1.at[e, d], recv_sem=r1.at[e, d],
            device_id=device, device_id_type=MESH)
        if start:
            cp.start()
            later.append(cp)
        else:
            cp.wait_recv()

    def relayed(d):
        if d == 4:
            relay(piece(4, 0), 4, 0, near[2], False)
            relay(piece(4, 1), 4, 1, near[6], False)
        else:
            relay(both(d), d, 0, near[1 if d == 3 else 7], False)

    later = []
    for i, d in enumerate(ORDER):
        if d == 0:
            for k in range(8):
                weights(k)
        if d == 3:
            tables()
            for k in range(8, KT):
                weights(k)
        if d == 0:
            mine.wait()
        if d in (3, 4, 5):
            relayed(d)
        else:
            recv_first(d)
        if d == 2:
            relay(both(2), 3, 0, near[1], True)
            relay(piece(2, 0), 4, 0, near[2], True)
        if d == 6:
            relay(both(6), 5, 0, near[7], True)
            relay(piece(6, 1), 4, 1, near[6], True)
        zz = plane(d)
        part = g.at[pl.ds(zz * 2, 2), rows(c, pos)]
        for j in (2, 1, 3):
            cp = pltpu.make_async_remote_copy(
                src_ref=part, dst_ref=part, send_sem=s2.at[j, d], recv_sem=r2.at[j, d],
                device_id=ring[j], device_id_type=MESH)
            cp.start()
            later.append(cp)

    def half(d, c_):
        ref = g.at[pl.ds((z + 8 - d) % 8 * 2, 2), pl.ds(pl.multiple_of(c_ * 128, 128), 128)]
        return pltpu.make_async_remote_copy(
            src_ref=ref, dst_ref=ref, send_sem=s3.at[d], recv_sem=r3.at[d],
            device_id=twin, device_id_type=MESH)

    for d in ORDER:
        zz = (z + 8 - d) % 8
        for j in (1, 3, 2):
            part = g.at[pl.ds(zz * 2, 2), rows(c, (pos + 4 - j) % 4)]
            pltpu.make_async_remote_copy(
                src_ref=part, dst_ref=part, send_sem=s2.at[j, d], recv_sem=r2.at[j, d],
                device_id=ring[j], device_id_type=MESH).wait_recv()
        later.append(half(d, c))
        later[-1].start()
    for d in ORDER:
        half(d, 1 - c).wait_recv()
    for cp in first + later:
        cp.wait_send()


def gather(row, cd, airr, own, amp, integ):
    smem = pl.BlockSpec(memory_space=pltpu.SMEM)
    vmem = pl.BlockSpec(memory_space=pltpu.VMEM)
    hbm = pl.BlockSpec(memory_space=pl.ANY)
    dma = pltpu.SemaphoreType.DMA
    return pl.pallas_call(
        gather_kernel,
        out_shape=(
            jax.ShapeDtypeStruct((16, SLOTS * 8, 128), F32),
            jax.ShapeDtypeStruct((KT, 128, 256), BF16),
            jax.ShapeDtypeStruct((8, 128), jnp.int32),
            jax.ShapeDtypeStruct((1,), jnp.int32),
        ),
        in_specs=[smem, smem, smem, vmem, vmem, hbm, hbm],
        out_specs=(vmem, vmem, vmem, smem),
        scratch_shapes=[
            pltpu.VMEM((SLOTS * 8, 128), F32),
            pltpu.VMEM((1, 128), jnp.int32),
            pltpu.SMEM((1, 128), jnp.int32),
            pltpu.VMEM((IRREPS * VB // 8, 8, KT * CD_TILE), F32),
            pltpu.VMEM((OWN_TILES * KT, ROW_TILE, CD_TILE), F32),
            dma, dma, dma, dma, dma((2, 8)), dma((2, 8)), dma((4, 8)), dma((4, 8)), dma((8,)), dma((8,)),
        ],
        compiler_params=pltpu.CompilerParams(
            collective_id=0, has_side_effects=True, vmem_limit_bytes=24 * 2**20),
        name="gather",
    )(row, cd, airr, row.reshape(1, TILES), own, amp, integ)


def product_kernel(tab, g, w, p, lhs, acc):
    p[ZEROT] = jnp.zeros((8, 128), F32)

    def label(lab, c):
        first = tab[T_START, lab]
        nr = tab[T_START, lab + 1] - first
        nk = tab[T_NK, lab]

        def rowsof(m, c):
            tiles = []
            for t in range(MT):
                ok = m * MT + t < nr
                v = tab[T_LST, first + jnp.minimum(m * MT + t, nr - 1)]
                tiles.append((jnp.where(ok, v & 255, DUMPT), v >> 8))
            acc[...] = jnp.zeros_like(acc)

            def depth(kc, c):
                ks = [kc * KC + h for h in range(KC)]
                have = [k < nk for k in ks]
                cols = [tab[T_KL, lab * KT + jnp.where(ok, k, 0)] for ok, k in zip(have, ks)]
                for t in range(MT):
                    off = tiles[t][1]
                    for h in range(KC):
                        src = g[jnp.minimum(off + jnp.where(have[h], ks[h], 0), 16 * SLOTS - 1)]
                        if h > 0:
                            src = jnp.where(have[h], src, 0.0)
                        lhs[t * 8:(t + 1) * 8, h * 128:(h + 1) * 128] = src
                a = lhs[...]
                hi = a.astype(BF16)
                lo = (a - hi.astype(F32)).astype(BF16)
                ww = jnp.concatenate([w[k] for k in cols], axis=0)
                big = jnp.dot(hi, ww, preferred_element_type=F32)
                small = jnp.dot(lo, ww[:, :128], preferred_element_type=F32)
                acc[...] += big[:, :128] + (big[:, 128:] + small)
                return c

            lax.fori_loop(0, (nk + KC - 1) // KC, depth, 0)
            for t in range(MT):
                p[tiles[t][0]] = acc[t * 8:(t + 1) * 8, :]
            return c

        return lax.fori_loop(0, (nr + MT - 1) // MT, rowsof, c)

    lax.fori_loop(0, IRREPS, label, 0)


def product(tab, g, w):
    smem = pl.BlockSpec(memory_space=pltpu.SMEM)
    vmem = pl.BlockSpec(memory_space=pltpu.VMEM)
    return pl.pallas_call(
        product_kernel,
        out_shape=jax.ShapeDtypeStruct((PT, 8, 128), F32),
        in_specs=[smem, vmem, vmem],
        out_specs=vmem,
        scratch_shapes=[pltpu.VMEM((MT * 8, KC * 128), F32), pltpu.VMEM((MT * 8, 128), F32)],
        compiler_params=pltpu.CompilerParams(vmem_limit_bytes=24 * 2**20),
        name="product",
    )(tab, g, w)


def owners_kernel(tab, p, out, send, loc_sem, ss, rs):
    me = lax.axis_index("slab")
    c = me % 2
    y = (me // 2) % 4
    xl = me // 8
    steps = [(a, b, e) for a, b in ((1, 2), (0, 2), (1, 1), (1, 3), (0, 1), (0, 3), (1, 0)) for e in (0, 1)] + [(0, 0, 1)]
    targets = [(xl + a) % 2 * 8 + (y + b) % 4 * 2 + (c + e) % 2 for a, b, e in steps]
    sources = [(xl + a) % 2 * 8 + (y + 4 - b) % 4 * 2 + (c + e) % 2 for a, b, e in steps]
    barrier = pltpu.get_barrier_semaphore()
    for o in targets:
        pl.semaphore_signal(barrier, inc=1, device_id={"slab": o}, device_id_type=MESH)

    def make(i, o):
        block = jnp.concatenate([p[tab[T_SRC + o // 8, o % 8 * CAP + q]] for q in range(CAP)], axis=0)
        send[i] = jnp.transpose(block)[:SENT]

    def copy(i, o, place):
        return pltpu.make_async_remote_copy(
            src_ref=send.at[i], dst_ref=out.at[place], send_sem=ss.at[i], recv_sem=rs.at[i],
            device_id={"slab": o}, device_id_type=MESH)

    EARLY = 4
    copies = []
    for i, o in enumerate(targets):
        make(i, o)
        if i == EARLY - 1:
            pl.semaphore_wait(barrier, 15)
            for j in range(EARLY):
                copies.append(copy(j, targets[j], me))
                copies[-1].start()
        elif i >= EARLY:
            copies.append(copy(i, o, me))
            copies[-1].start()
    make(15, me)
    local = pltpu.make_async_copy(send.at[15], out.at[me], loc_sem)
    local.start()
    for i, o in enumerate(sources):
        copy(i, o, o).wait_recv()
    for cp in copies:
        cp.wait_send()
    local.wait()


def owners(tab, p):
    smem = pl.BlockSpec(memory_space=pltpu.SMEM)
    vmem = pl.BlockSpec(memory_space=pltpu.VMEM)
    dma = pltpu.SemaphoreType.DMA
    return pl.pallas_call(
        owners_kernel,
        out_shape=jax.ShapeDtypeStruct((16, SENT, 128), F32),
        in_specs=[smem, vmem],
        out_specs=vmem,
        scratch_shapes=[pltpu.VMEM((16, SENT, 128), F32), dma, dma((16,)), dma((16,))],
        compiler_params=pltpu.CompilerParams(
            collective_id=1, has_side_effects=True, vmem_limit_bytes=24 * 2**20),
        name="owners",
    )(tab, p)


def expand_kernel(airr, tab, arrived, out, stage, sems):
    blk = lax.axis_index("blk")
    lab = tab[T_LAB:T_LAB + 1, :]
    upper = lax.broadcasted_iota(jnp.int32, (8, 128), 0) < 4

    def one(s, c):
        want = lab ^ airr[s, blk]
        block = arrived[s]
        block = jnp.concatenate([block, block[0:4]], axis=0)
        moved = jnp.concatenate([block[100:104], block[0:100]], axis=0)
        for m in range(IRREPS // 2):
            even = want == 2 * m
            odd = want == 2 * m + 1
            base = 2 * VB * m
            stage[s, base:base + 96, :] = jnp.where(even, block[:96], 0.0)
            stage[s, base + 96:base + 104, :] = jnp.where(
                upper, jnp.where(even, block[96:], 0.0), jnp.where(odd, moved[:8], 0.0))
            stage[s, base + 104:base + 200, :] = jnp.where(odd, moved[8:], 0.0)
        pltpu.make_async_copy(stage.at[s], out.at[s], sems.at[s]).start()
        return c

    lax.fori_loop(0, 16, one, 0)
    for s in range(16):
        pltpu.make_async_copy(stage.at[s], out.at[s], sems.at[s]).wait()


def expand(airr, tab, arrived):
    return pl.pallas_call(
        expand_kernel,
        out_shape=jax.ShapeDtypeStruct((16, IRREPS * VB, 128), F32),
        in_specs=[pl.BlockSpec(memory_space=pltpu.SMEM)] + [pl.BlockSpec(memory_space=pltpu.VMEM)] * 2,
        out_specs=pl.BlockSpec(memory_space=pl.ANY),
        scratch_shapes=[pltpu.VMEM((16, IRREPS * VB, 128), F32), pltpu.SemaphoreType.DMA((16,))],
        compiler_params=pltpu.CompilerParams(vmem_limit_bytes=40 * 2**20),
        name="expand",
    )(airr, tab, arrived)


def dense(amplitude, integ, row, cd, airr, tab):
    slab = lax.axis_index("slab")
    blk = lax.axis_index("blk")
    own_a = airr[slab, blk]
    copies = jnp.broadcast_to(amplitude[None], (16,) + amplitude.shape)
    piece = lax.all_to_all(copies, "blk", split_axis=0, concat_axis=0, tiled=True).reshape(-1, KT * CD_TILE)
    cd_cols = jnp.repeat(cd, CD_TILE)
    labels = jnp.repeat(row, ROW_TILE)
    coupled = jnp.where(labels[:, None] == cd_cols[None, :], piece, 0.0)
    blocks = integ.reshape(IRREPS, VB, KT * CD_TILE)
    want = cd_cols ^ own_a
    kept = jnp.sum(jnp.where(want[None, None, :] == jnp.arange(IRREPS)[:, None, None], blocks, 0.0), axis=0)
    prod = jnp.dot(coupled, kept.T, precision=lax.Precision.HIGHEST, preferred_element_type=F32)
    prod = jnp.concatenate([prod.reshape(TILES, ROW_TILE, VB), jnp.zeros((1, ROW_TILE, VB), F32)], axis=0)
    packed = jnp.take(prod, tab[T_SRC:T_SRC + 2].reshape(-1), axis=0).reshape(16, CAP * ROW_TILE, VB)
    arrived = lax.all_to_all(packed, "slab", split_axis=0, concat_axis=0, tiled=True)
    arrived = jnp.transpose(arrived, (0, 2, 1))
    return arrived


def shards(amplitude, integrals, row, cd, airr, owner):
    integ = integrals.reshape(KT * CD_TILE, IRREPS * VB).T
    amp = amplitude.reshape(OWN_TILES, ROW_TILE, KT, CD_TILE).transpose(0, 2, 1, 3)
    g, w, tab, fit = gather(
        row, cd, airr, owner.reshape(1, TILES), amp.reshape(OWN_TILES * KT, ROW_TILE, CD_TILE),
        integ.reshape(IRREPS * VB // 8, 8, KT * CD_TILE))

    p = product(tab, g.reshape(16 * SLOTS, 8, 128), w)

    def fast(amplitude, integ, row, cd, airr, tab, p):
        return owners(tab, p)

    def slow(amplitude, integ, row, cd, airr, tab, p):
        return dense(amplitude, integ, row, cd, airr, tab)

    arrived = lax.cond(fit[0] == 1, fast, slow, amplitude, integ, row, cd, airr, tab, p)
    out = expand(airr, tab, arrived)
    return jnp.transpose(out, (2, 0, 1)).reshape(CAP * ROW_TILE, 16, 1, IRREPS * VB)


def solution(mesh):
    return jax.shard_map(
        shards,
        mesh=mesh,
        in_specs=(P("blk", None), P(None, "slab", "blk", None), P(), P(), P(), P()),
        out_specs=P("slab", None, "blk", None),
        check_vma=False,
    )
```

```python
import functools

import jax
import jax.numpy as jnp
from jax import lax
from jax.experimental import pallas as pl
from jax.experimental.pallas import tpu as pltpu
from jax.sharding import PartitionSpec as P

IRREPS = 8
CD_TILE = 128
ROW_TILE = 8
TILES = 128
KT = 16
OWN_TILES = 8
SLOTS = 32
CAP = 16
VB = 100
VP = 104
ZEROT = 128
DUMPT = 129
PT = 136
SENT = 100
MT = 24
KC = 2
GATHERED = 20
T_LST = 0
T_SRC = 1
T_START = 3
T_KL = 4
T_NK = 5
T_LAB = 6

MESH = pl.DeviceIdType.MESH
F32 = jnp.float32
BF16 = jnp.bfloat16


ORDER = (0, 2, 6, 1, 7, 3, 5, 4)


def gather_kernel(row, cd, airr, row_v, own_v, amp_hbm, integ, g, w, tab, fit, comp, found, found_s, raw, amp, amp_sem, found_sem, loc_sem, raw_sem, s1, r1, s2, r2, s3, r3):
    slab = lax.axis_index("slab")
    blk = lax.axis_index("blk")
    c = slab % 2
    y = (slab // 2) % 4
    xl = slab // 8
    z = blk // 2
    xh = blk % 2
    x = xh * 2 + xl
    pos = (1 - c) * x + c * y

    def dev(x_, y_, z_, c_):
        return {"slab": (x_ % 2) * 8 + y_ * 2 + c_, "blk": z_ * 2 + x_ // 2}

    amp_copy = pltpu.make_async_copy(amp_hbm, amp, amp_sem)
    amp_copy.start()
    raw_copy = pltpu.make_async_copy(integ, raw, raw_sem)
    raw_copy.start()

    near = {d: dev(x, y, (z + d) % 8, c) for d in (1, 7, 2, 6)}
    cross = {d: dev(3 - x, y, (z + d) % 8, c) for d in (0, 1, 7, 2, 6)}
    ring = [None] + [dev((x + (1 - c) * j) % 4, (y + c * j) % 4, z, c) for j in range(1, 4)]
    twin = dev(x, y, z, 1 - c)

    barrier = pltpu.get_barrier_semaphore()
    peers = list(near.values()) + list(cross.values()) + ring[1:] + [twin]
    for peer in peers:
        pl.semaphore_signal(barrier, inc=1, device_id=peer, device_id_type=MESH)

    def rows(c_, p_):
        return pl.ds(pl.multiple_of(c_ * 128 + p_ * 32, 32), 32)

    labs = [cd[k] for k in range(KT)]
    sub = lax.broadcasted_iota(jnp.int32, (128, 128), 0)
    lane = lax.broadcasted_iota(jnp.int32, (128, 128), 1)
    one_lane = lax.broadcasted_iota(jnp.int32, (1, 128), 1)

    def coupled_at(place):
        left = jnp.zeros(place.shape, jnp.int32)
        for t in range(OWN_TILES):
            left = jnp.where(place // KT == t, row[blk * OWN_TILES + t], left)
        right = jnp.zeros(place.shape, jnp.int32)
        for k in range(KT):
            right = jnp.where(place % KT == k, labs[k], right)
        return left == right

    down = coupled_at(lax.broadcasted_iota(jnp.int32, (128, 1), 0))
    across = jnp.where(coupled_at(one_lane), 1, 0)
    ahead = jnp.sum(jnp.where(lane < sub, across, 0), axis=1, keepdims=True)
    place = jnp.where(down, ahead, -1)
    found[...] = jnp.sum(jnp.where(place == lane, sub, 0), axis=0, keepdims=True)
    move = pltpu.make_async_copy(found, found_s, found_sem)
    move.start()
    move.wait()
    amp_copy.wait()
    for j in range(SLOTS):
        comp[j * 8:(j + 1) * 8, :] = amp[found_s[0, j]]

    mine = pltpu.make_async_copy(comp.at[rows(c, pos)], g.at[blk, rows(c, pos)], loc_sem)
    mine.start()
    pl.semaphore_wait(barrier, len(peers))

    cross_pos = (1 - c) * (3 - x) + c * y
    first = []
    for d in (2, 6, 0, 1, 7):
        if d != 0:
            cp = pltpu.make_async_remote_copy(
                src_ref=comp.at[rows(c, pos)], dst_ref=g.at[blk, rows(c, pos)],
                send_sem=s1.at[0, d], recv_sem=r1.at[0, d],
                device_id=near[d], device_id_type=MESH)
            cp.start()
            first.append(cp)
        cp = pltpu.make_async_remote_copy(
            src_ref=comp.at[rows(c, cross_pos)], dst_ref=g.at[blk, rows(c, cross_pos)],
            send_sem=s1.at[1, d], recv_sem=r1.at[1, d],
            device_id=cross[d], device_id_type=MESH)
        cp.start()
        first.append(cp)

    raw_copy.wait()
    own_a = airr[slab, blk]

    def tables():
        row_l = row_v[...]
        own_l = own_v[...]
        diag = sub == lane
        row_c = jnp.sum(jnp.where(diag, row_l, 0), axis=1, keepdims=True)
        own_c = jnp.sum(jnp.where(diag, own_l, 0), axis=1, keepdims=True)
        before = lane < sub
        sub_c = lax.broadcasted_iota(jnp.int32, (128, 1), 0)
        rank = jnp.sum(jnp.where((own_l == own_c) & before, 1, 0), axis=1, keepdims=True)
        target = own_c * CAP + rank
        for h in range(2):
            tab[T_SRC + h:T_SRC + h + 1, :] = ZEROT + jnp.sum(
                jnp.where(target == lane + h * 128, sub - ZEROT, 0), axis=0, keepdims=True)
        tab[T_LAB:T_LAB + 1, :] = jnp.sum(
            jnp.where(target == slab * CAP + lane // ROW_TILE, row_c, 0), axis=0, keepdims=True)
        order = jnp.sum(jnp.where((row_l < row_c) | ((row_l == row_c) & before), 1, 0), axis=1, keepdims=True)
        nk_l = jnp.zeros((1, 128), jnp.int32)
        nk_c = jnp.zeros((128, 1), jnp.int32)
        nk_of = jnp.zeros((1, 128), jnp.int32)
        list_l = jnp.zeros((1, 128), jnp.int32)
        for k in range(KT):
            nk_l = nk_l + jnp.where(row_l == labs[k], 1, 0)
            nk_c = nk_c + jnp.where(row_c == labs[k], 1, 0)
            nk_of = nk_of + jnp.where(one_lane == labs[k], 1, 0)
            kap = jnp.int32(0)
            for other in range(k):
                kap = kap + jnp.where(labs[other] == labs[k], 1, 0)
            list_l = list_l + jnp.where(one_lane == labs[k] * KT + kap, k, 0)
        same = (lane // OWN_TILES == sub // OWN_TILES) & before
        inside = jnp.sum(jnp.where(same, nk_l, 0), axis=1, keepdims=True)
        value = sub_c + 256 * (SLOTS * (sub_c // OWN_TILES) + inside)
        tab[T_LST:T_LST + 1, :] = jnp.sum(jnp.where(order == lane, value, 0), axis=0, keepdims=True)
        tab[T_START:T_START + 1, :] = jnp.sum(jnp.where(row_c < lane, 1, 0), axis=0, keepdims=True)
        tab[T_KL:T_KL + 1, :] = list_l
        tab[T_NK:T_NK + 1, :] = nk_of
        tab[7:8, :] = jnp.zeros((1, 128), jnp.int32)
        fit[0] = jnp.where(jnp.max(inside + nk_c) <= SLOTS, 1, 0)

    def weights(k):
        beta = labs[k] ^ own_a
        odd = beta & 1
        start = beta * 12 + beta // 2
        block = jnp.concatenate([raw[start + i, :, k * 128:(k + 1) * 128] for i in range(VP // 8)], axis=0)
        moved = jnp.concatenate([block[4:], block[:4]], axis=0)
        block = jnp.where(odd == 1, moved, block)
        block = jnp.concatenate([block, jnp.zeros((128 - VP, 128), F32)], axis=0)
        block = jnp.transpose(block)
        hi = block.astype(BF16)
        lo = (block - hi.astype(F32)).astype(BF16)
        w[k, :, 0:128] = hi
        w[k, :, 128:256] = lo

    def plane(d):
        return (z + 8 - d) % 8

    def piece(d, e):
        return g.at[plane(d) * 2 + (xh if e == 0 else 1 - xh), rows(c, pos)]

    def both(d):
        return g.at[pl.ds(plane(d) * 2, 2), rows(c, pos)]

    def recv_first(d):
        for e in ((1,) if d == 0 else (0, 1)):
            pltpu.make_async_remote_copy(
                src_ref=piece(d, e), dst_ref=piece(d, e), send_sem=s1.at[e, d], recv_sem=r1.at[e, d],
                device_id=twin, device_id_type=MESH).wait_recv()

    def relay(ref, d, e, device, start):
        cp = pltpu.make_async_remote_copy(
            src_ref=ref, dst_ref=ref, send_sem=s1.at[e, d], recv_sem=r1.at[e, d],
            device_id=device, device_id_type=MESH)
        if start:
            cp.start()
            later.append(cp)
        else:
            cp.wait_recv()

    def relayed(d):
        if d == 4:
            relay(piece(4, 0), 4, 0, near[2], False)
            relay(piece(4, 1), 4, 1, near[6], False)
        else:
            relay(both(d), d, 0, near[1 if d == 3 else 7], False)

    later = []
    for i, d in enumerate(ORDER):
        if d == 0:
            for k in range(8):
                weights(k)
        if d == 3:
            tables()
            for k in range(8, KT):
                weights(k)
        if d == 0:
            mine.wait()
        if d in (3, 4, 5):
            relayed(d)
        else:
            recv_first(d)
        if d == 2:
            relay(both(2), 3, 0, near[1], True)
            relay(piece(2, 0), 4, 0, near[2], True)
        if d == 6:
            relay(both(6), 5, 0, near[7], True)
            relay(piece(6, 1), 4, 1, near[6], True)
        zz = plane(d)
        part = g.at[pl.ds(zz * 2, 2), rows(c, pos)]
        for j in (2, 1, 3):
            cp = pltpu.make_async_remote_copy(
                src_ref=part, dst_ref=part, send_sem=s2.at[j, d], recv_sem=r2.at[j, d],
                device_id=ring[j], device_id_type=MESH)
            cp.start()
            later.append(cp)

    def half(d, c_):
        ref = g.at[pl.ds((z + 8 - d) % 8 * 2, 2), pl.ds(pl.multiple_of(c_ * 128, 128), 128)]
        return pltpu.make_async_remote_copy(
            src_ref=ref, dst_ref=ref, send_sem=s3.at[d], recv_sem=r3.at[d],
            device_id=twin, device_id_type=MESH)

    for d in ORDER:
        zz = (z + 8 - d) % 8
        for j in (1, 3, 2):
            part = g.at[pl.ds(zz * 2, 2), rows(c, (pos + 4 - j) % 4)]
            pltpu.make_async_remote_copy(
                src_ref=part, dst_ref=part, send_sem=s2.at[j, d], recv_sem=r2.at[j, d],
                device_id=ring[j], device_id_type=MESH).wait_recv()
        later.append(half(d, c))
        later[-1].start()
    for d in ORDER:
        half(d, 1 - c).wait_recv()
    for cp in first + later:
        cp.wait_send()


def gather(row, cd, airr, own, amp, integ):
    smem = pl.BlockSpec(memory_space=pltpu.SMEM)
    vmem = pl.BlockSpec(memory_space=pltpu.VMEM)
    hbm = pl.BlockSpec(memory_space=pl.ANY)
    dma = pltpu.SemaphoreType.DMA
    return pl.pallas_call(
        gather_kernel,
        out_shape=(
            jax.ShapeDtypeStruct((GATHERED, SLOTS * 8, 128), F32),
            jax.ShapeDtypeStruct((KT, 128, 256), BF16),
            jax.ShapeDtypeStruct((8, 128), jnp.int32),
            jax.ShapeDtypeStruct((1,), jnp.int32),
        ),
        in_specs=[smem, smem, smem, vmem, vmem, hbm, hbm],
        out_specs=(vmem, vmem, vmem, smem),
        scratch_shapes=[
            pltpu.VMEM((SLOTS * 8, 128), F32),
            pltpu.VMEM((1, 128), jnp.int32),
            pltpu.SMEM((1, 128), jnp.int32),
            pltpu.VMEM((IRREPS * VB // 8, 8, KT * CD_TILE), F32),
            pltpu.VMEM((OWN_TILES * KT, ROW_TILE, CD_TILE), F32),
            dma, dma, dma, dma, dma((2, 8)), dma((2, 8)), dma((4, 8)), dma((4, 8)), dma((8,)), dma((8,)),
        ],
        compiler_params=pltpu.CompilerParams(
            collective_id=0, has_side_effects=True, vmem_limit_bytes=24 * 2**20),
        name="gather",
    )(row, cd, airr, row.reshape(1, TILES), own, amp, integ)


def product_kernel(tab, g, w, p, acc):
    p[ZEROT] = jnp.zeros((8, 128), F32)

    def label(lab, c):
        first = tab[T_START, lab]
        nr = tab[T_START, lab + 1] - first
        nk = tab[T_NK, lab]

        def rowsof(m, c):
            tiles = []
            for t in range(MT):
                ok = m * MT + t < nr
                v = tab[T_LST, first + jnp.minimum(m * MT + t, nr - 1)]
                tiles.append((jnp.where(ok, v & 255, DUMPT), v >> 8))
            acc[...] = jnp.zeros_like(acc)

            def depth(kc, c):
                ks = [kc * KC + h for h in range(KC)]
                have = [k < nk for k in ks]
                cols = [tab[T_KL, lab * KT + jnp.where(ok, k, 0)] for ok, k in zip(have, ks)]
                at = [jnp.where(ok, k, 0) for ok, k in zip(have, ks)]
                parts = []
                for h in range(KC):
                    part = jnp.concatenate([g[tiles[t][1] + at[h]] for t in range(MT)], axis=0)
                    parts.append(part if h == 0 else jnp.where(have[h], part, 0.0))
                a = jnp.concatenate(parts, axis=1)
                hi = a.astype(BF16)
                lo = (a - hi.astype(F32)).astype(BF16)
                ww = jnp.concatenate([w[k] for k in cols], axis=0)
                big = jnp.dot(hi, ww, preferred_element_type=F32)
                small = jnp.dot(lo, ww[:, :128], preferred_element_type=F32)
                acc[...] += big[:, :128] + (big[:, 128:] + small)
                return c

            lax.fori_loop(0, (nk + KC - 1) // KC, depth, 0)
            for t in range(MT):
                p[tiles[t][0]] = acc[t * 8:(t + 1) * 8, :]
            return c

        return lax.fori_loop(0, (nr + MT - 1) // MT, rowsof, c)

    lax.fori_loop(0, IRREPS, label, 0)


def product(tab, g, w):
    smem = pl.BlockSpec(memory_space=pltpu.SMEM)
    vmem = pl.BlockSpec(memory_space=pltpu.VMEM)
    return pl.pallas_call(
        product_kernel,
        out_shape=jax.ShapeDtypeStruct((PT, 8, 128), F32),
        in_specs=[smem, vmem, vmem],
        out_specs=vmem,
        scratch_shapes=[pltpu.VMEM((MT * 8, 128), F32)],
        compiler_params=pltpu.CompilerParams(vmem_limit_bytes=24 * 2**20),
        name="product",
    )(tab, g, w)


def owners_kernel(tab, p, out, send, loc_sem, ss, rs):
    me = lax.axis_index("slab")
    c = me % 2
    y = (me // 2) % 4
    xl = me // 8
    steps = [(a, b, e) for a, b in ((1, 2), (0, 2), (1, 1), (1, 3), (0, 1), (0, 3), (1, 0)) for e in (0, 1)] + [(0, 0, 1)]
    targets = [(xl + a) % 2 * 8 + (y + b) % 4 * 2 + (c + e) % 2 for a, b, e in steps]
    sources = [(xl + a) % 2 * 8 + (y + 4 - b) % 4 * 2 + (c + e) % 2 for a, b, e in steps]
    barrier = pltpu.get_barrier_semaphore()
    for o in targets:
        pl.semaphore_signal(barrier, inc=1, device_id={"slab": o}, device_id_type=MESH)

    def make(i, o):
        block = jnp.concatenate([p[tab[T_SRC + o // 8, o % 8 * CAP + q]] for q in range(CAP)], axis=0)
        send[i] = jnp.transpose(block)[:SENT]

    def copy(i, o, place):
        return pltpu.make_async_remote_copy(
            src_ref=send.at[i], dst_ref=out.at[place], send_sem=ss.at[i], recv_sem=rs.at[i],
            device_id={"slab": o}, device_id_type=MESH)

    EARLY = 4
    copies = []
    for i, o in enumerate(targets):
        make(i, o)
        if i == EARLY - 1:
            pl.semaphore_wait(barrier, 15)
            for j in range(EARLY):
                copies.append(copy(j, targets[j], me))
                copies[-1].start()
        elif i >= EARLY:
            copies.append(copy(i, o, me))
            copies[-1].start()
    make(15, me)
    local = pltpu.make_async_copy(send.at[15], out.at[me], loc_sem)
    local.start()
    for i, o in enumerate(sources):
        copy(i, o, o).wait_recv()
    for cp in copies:
        cp.wait_send()
    local.wait()


def owners(tab, p):
    smem = pl.BlockSpec(memory_space=pltpu.SMEM)
    vmem = pl.BlockSpec(memory_space=pltpu.VMEM)
    dma = pltpu.SemaphoreType.DMA
    return pl.pallas_call(
        owners_kernel,
        out_shape=jax.ShapeDtypeStruct((16, SENT, 128), F32),
        in_specs=[smem, vmem],
        out_specs=vmem,
        scratch_shapes=[pltpu.VMEM((16, SENT, 128), F32), dma, dma((16,)), dma((16,))],
        compiler_params=pltpu.CompilerParams(
            collective_id=1, has_side_effects=True, vmem_limit_bytes=24 * 2**20),
        name="owners",
    )(tab, p)


def expand_kernel(airr, tab, arrived, out, stage, sems):
    blk = lax.axis_index("blk")
    lab = tab[T_LAB:T_LAB + 1, :]
    upper = lax.broadcasted_iota(jnp.int32, (8, 128), 0) < 4

    def one(s, c):
        want = lab ^ airr[s, blk]
        block = arrived[s]
        block = jnp.concatenate([block, block[0:4]], axis=0)
        moved = jnp.concatenate([block[100:104], block[0:100]], axis=0)
        for m in range(IRREPS // 2):
            even = want == 2 * m
            odd = want == 2 * m + 1
            base = 2 * VB * m
            stage[s, base:base + 96, :] = jnp.where(even, block[:96], 0.0)
            stage[s, base + 96:base + 104, :] = jnp.where(
                upper, jnp.where(even, block[96:], 0.0), jnp.where(odd, moved[:8], 0.0))
            stage[s, base + 104:base + 200, :] = jnp.where(odd, moved[8:], 0.0)
        pltpu.make_async_copy(stage.at[s], out.at[s], sems.at[s]).start()
        return c

    lax.fori_loop(0, 16, one, 0)
    for s in range(16):
        pltpu.make_async_copy(stage.at[s], out.at[s], sems.at[s]).wait()


def expand(airr, tab, arrived):
    return pl.pallas_call(
        expand_kernel,
        out_shape=jax.ShapeDtypeStruct((16, IRREPS * VB, 128), F32),
        in_specs=[pl.BlockSpec(memory_space=pltpu.SMEM)] + [pl.BlockSpec(memory_space=pltpu.VMEM)] * 2,
        out_specs=pl.BlockSpec(memory_space=pl.ANY),
        scratch_shapes=[pltpu.VMEM((16, IRREPS * VB, 128), F32), pltpu.SemaphoreType.DMA((16,))],
        compiler_params=pltpu.CompilerParams(vmem_limit_bytes=40 * 2**20),
        name="expand",
    )(airr, tab, arrived)


def dense(amplitude, integ, row, cd, airr, owner):
    slab = lax.axis_index("slab")
    blk = lax.axis_index("blk")
    own_a = airr[slab, blk]
    copies = jnp.broadcast_to(amplitude[None], (16,) + amplitude.shape)
    piece = lax.all_to_all(copies, "blk", split_axis=0, concat_axis=0, tiled=True).reshape(-1, KT * CD_TILE)
    cd_cols = jnp.repeat(cd, CD_TILE)
    labels = jnp.repeat(row, ROW_TILE)
    coupled = jnp.where(labels[:, None] == cd_cols[None, :], piece, 0.0)
    blocks = integ.reshape(IRREPS, VB, KT * CD_TILE)
    want = cd_cols ^ own_a
    kept = jnp.sum(jnp.where(want[None, None, :] == jnp.arange(IRREPS)[:, None, None], blocks, 0.0), axis=0)
    prod = jnp.dot(coupled, kept.T, precision=lax.Precision.HIGHEST, preferred_element_type=F32)
    prod = jnp.concatenate([prod.reshape(TILES, ROW_TILE, VB), jnp.zeros((1, ROW_TILE, VB), F32)], axis=0)
    own = owner[:, 0]
    tiles = jnp.arange(TILES, dtype=jnp.int32)
    ahead = (own[:, None] == own[None, :]) & (tiles[None, :] < tiles[:, None])
    target = own * CAP + jnp.sum(ahead.astype(jnp.int32), axis=1)
    hit = target[None, :] == jnp.arange(16 * CAP, dtype=jnp.int32)[:, None]
    source = ZEROT + jnp.sum(jnp.where(hit, tiles[None, :] - ZEROT, 0), axis=1)
    packed = jnp.take(prod, source, axis=0).reshape(16, CAP * ROW_TILE, VB)
    arrived = lax.all_to_all(packed, "slab", split_axis=0, concat_axis=0, tiled=True)
    arrived = jnp.transpose(arrived, (0, 2, 1))
    return arrived


def shards(amplitude, integrals, row, cd, airr, owner):
    integ = integrals.reshape(KT * CD_TILE, IRREPS * VB).T
    amp = amplitude.reshape(OWN_TILES, ROW_TILE, KT, CD_TILE).transpose(0, 2, 1, 3)
    g, w, tab, fit = gather(
        row, cd, airr, owner.reshape(1, TILES), amp.reshape(OWN_TILES * KT, ROW_TILE, CD_TILE),
        integ.reshape(IRREPS * VB // 8, 8, KT * CD_TILE))

    p = product(tab, g.reshape(GATHERED * SLOTS, 8, 128), w)

    def fast(amplitude, integ, row, cd, airr, owner, tab, p):
        return owners(tab, p)

    def slow(amplitude, integ, row, cd, airr, owner, tab, p):
        return dense(amplitude, integ, row, cd, airr, owner)

    arrived = lax.cond(fit[0] == 1, fast, slow, amplitude, integ, row, cd, airr, owner, tab, p)
    out = expand(airr, tab, arrived)
    return jnp.transpose(out, (2, 0, 1)).reshape(CAP * ROW_TILE, 16, 1, IRREPS * VB)


def solution(mesh):
    return jax.shard_map(
        shards,
        mesh=mesh,
        in_specs=(P("blk", None), P(None, "slab", "blk", None), P(), P(), P(), P()),
        out_specs=P("slab", None, "blk", None),
        check_vma=False,
    )
```

```python
import functools

import jax
import jax.numpy as jnp
from jax import lax
from jax.experimental import pallas as pl
from jax.experimental.pallas import tpu as pltpu
from jax.sharding import PartitionSpec as P

IRREPS = 8
CD_TILE = 128
ROW_TILE = 8
TILES = 128
KT = 16
OWN_TILES = 8
SLOTS = 32
CAP = 16
VB = 100
VP = 104
ZEROT = 128
DUMPT = 129
PT = 136
SENT = 100
MT = 24
KC = 2
GATHERED = 20
T_LST = 0
T_SRC = 1
T_START = 3
T_KL = 4
T_NK = 5
T_LAB = 6

MESH = pl.DeviceIdType.MESH
F32 = jnp.float32
BF16 = jnp.bfloat16


ORDER = (0, 2, 6, 1, 7, 3, 5, 4)


def gather_kernel(row, cd, airr, row_v, own_v, amp_hbm, integ, g, w, tab, fit, comp, found, found_s, raw, amp, amp_sem, found_sem, loc_sem, raw_sem, s1, r1, s2, r2, s3, r3):
    slab = lax.axis_index("slab")
    blk = lax.axis_index("blk")
    c = slab % 2
    y = (slab // 2) % 4
    xl = slab // 8
    z = blk // 2
    xh = blk % 2
    x = xh * 2 + xl
    pos = (1 - c) * x + c * y

    def dev(x_, y_, z_, c_):
        return {"slab": (x_ % 2) * 8 + y_ * 2 + c_, "blk": z_ * 2 + x_ // 2}

    amp_copy = pltpu.make_async_copy(amp_hbm, amp, amp_sem)
    amp_copy.start()
    raw_copy = pltpu.make_async_copy(integ, raw, raw_sem)
    raw_copy.start()

    near = {d: dev(x, y, (z + d) % 8, c) for d in (1, 7, 2, 6)}
    cross = {d: dev(3 - x, y, (z + d) % 8, c) for d in (0, 1, 7, 2, 6)}
    ring = [None] + [dev((x + (1 - c) * j) % 4, (y + c * j) % 4, z, c) for j in range(1, 4)]
    twin = dev(x, y, z, 1 - c)

    barrier = pltpu.get_barrier_semaphore()
    peers = list(near.values()) + list(cross.values()) + ring[1:] + [twin]
    for peer in peers:
        pl.semaphore_signal(barrier, inc=1, device_id=peer, device_id_type=MESH)

    def rows(c_, p_):
        return pl.ds(pl.multiple_of(c_ * 128 + p_ * 32, 32), 32)

    labs = [cd[k] for k in range(KT)]
    sub = lax.broadcasted_iota(jnp.int32, (128, 128), 0)
    lane = lax.broadcasted_iota(jnp.int32, (128, 128), 1)
    one_lane = lax.broadcasted_iota(jnp.int32, (1, 128), 1)

    def coupled_at(place):
        left = jnp.zeros(place.shape, jnp.int32)
        for t in range(OWN_TILES):
            left = jnp.where(place // KT == t, row[blk * OWN_TILES + t], left)
        right = jnp.zeros(place.shape, jnp.int32)
        for k in range(KT):
            right = jnp.where(place % KT == k, labs[k], right)
        return left == right

    down = coupled_at(lax.broadcasted_iota(jnp.int32, (128, 1), 0))
    across = jnp.where(coupled_at(one_lane), 1, 0)
    ahead = jnp.sum(jnp.where(lane < sub, across, 0), axis=1, keepdims=True)
    place = jnp.where(down, ahead, -1)
    found[...] = jnp.sum(jnp.where(place == lane, sub, 0), axis=0, keepdims=True)
    move = pltpu.make_async_copy(found, found_s, found_sem)
    move.start()
    move.wait()
    amp_copy.wait()
    for j in range(SLOTS):
        comp[j * 8:(j + 1) * 8, :] = amp[found_s[0, j]]

    mine = pltpu.make_async_copy(comp.at[rows(c, pos)], g.at[blk, rows(c, pos)], loc_sem)
    mine.start()
    pl.semaphore_wait(barrier, len(peers))

    cross_pos = (1 - c) * (3 - x) + c * y
    first = []
    for d in (2, 6, 0, 1, 7):
        if d != 0:
            cp = pltpu.make_async_remote_copy(
                src_ref=comp.at[rows(c, pos)], dst_ref=g.at[blk, rows(c, pos)],
                send_sem=s1.at[0, d], recv_sem=r1.at[0, d],
                device_id=near[d], device_id_type=MESH)
            cp.start()
            first.append(cp)
        cp = pltpu.make_async_remote_copy(
            src_ref=comp.at[rows(c, cross_pos)], dst_ref=g.at[blk, rows(c, cross_pos)],
            send_sem=s1.at[1, d], recv_sem=r1.at[1, d],
            device_id=cross[d], device_id_type=MESH)
        cp.start()
        first.append(cp)

    raw_copy.wait()
    own_a = airr[slab, blk]

    def tables():
        row_l = row_v[...]
        own_l = own_v[...]
        diag = sub == lane
        row_c = jnp.sum(jnp.where(diag, row_l, 0), axis=1, keepdims=True)
        own_c = jnp.sum(jnp.where(diag, own_l, 0), axis=1, keepdims=True)
        before = lane < sub
        sub_c = lax.broadcasted_iota(jnp.int32, (128, 1), 0)
        rank = jnp.sum(jnp.where((own_l == own_c) & before, 1, 0), axis=1, keepdims=True)
        target = own_c * CAP + rank
        for h in range(2):
            tab[T_SRC + h:T_SRC + h + 1, :] = ZEROT + jnp.sum(
                jnp.where(target == lane + h * 128, sub - ZEROT, 0), axis=0, keepdims=True)
        tab[T_LAB:T_LAB + 1, :] = jnp.sum(
            jnp.where(target == slab * CAP + lane // ROW_TILE, row_c, 0), axis=0, keepdims=True)
        order = jnp.sum(jnp.where((row_l < row_c) | ((row_l == row_c) & before), 1, 0), axis=1, keepdims=True)
        nk_l = jnp.zeros((1, 128), jnp.int32)
        nk_c = jnp.zeros((128, 1), jnp.int32)
        nk_of = jnp.zeros((1, 128), jnp.int32)
        list_l = jnp.zeros((1, 128), jnp.int32)
        for k in range(KT):
            nk_l = nk_l + jnp.where(row_l == labs[k], 1, 0)
            nk_c = nk_c + jnp.where(row_c == labs[k], 1, 0)
            nk_of = nk_of + jnp.where(one_lane == labs[k], 1, 0)
            kap = jnp.int32(0)
            for other in range(k):
                kap = kap + jnp.where(labs[other] == labs[k], 1, 0)
            list_l = list_l + jnp.where(one_lane == labs[k] * KT + kap, k, 0)
        same = (lane // OWN_TILES == sub // OWN_TILES) & before
        inside = jnp.sum(jnp.where(same, nk_l, 0), axis=1, keepdims=True)
        value = sub_c + 256 * (SLOTS * (sub_c // OWN_TILES) + inside)
        tab[T_LST:T_LST + 1, :] = jnp.sum(jnp.where(order == lane, value, 0), axis=0, keepdims=True)
        tab[T_START:T_START + 1, :] = jnp.sum(jnp.where(row_c < lane, 1, 0), axis=0, keepdims=True)
        tab[T_KL:T_KL + 1, :] = list_l
        tab[T_NK:T_NK + 1, :] = nk_of
        tab[7:8, :] = jnp.zeros((1, 128), jnp.int32)
        fit[0] = jnp.where(jnp.max(inside + nk_c) <= SLOTS, 1, 0)

    def weights(k):
        beta = labs[k] ^ own_a
        odd = beta & 1
        start = beta * 12 + beta // 2
        block = jnp.concatenate([raw[start + i, :, k * 128:(k + 1) * 128] for i in range(VP // 8)], axis=0)
        moved = jnp.concatenate([block[4:], block[:4]], axis=0)
        block = jnp.where(odd == 1, moved, block)
        block = jnp.concatenate([block, jnp.zeros((128 - VP, 128), F32)], axis=0)
        block = jnp.transpose(block)
        hi = block.astype(BF16)
        lo = (block - hi.astype(F32)).astype(BF16)
        w[k, :, 0:128] = hi
        w[k, :, 128:256] = lo

    def plane(d):
        return (z + 8 - d) % 8

    def piece(d, e):
        return g.at[plane(d) * 2 + (xh if e == 0 else 1 - xh), rows(c, pos)]

    def both(d):
        return g.at[pl.ds(plane(d) * 2, 2), rows(c, pos)]

    def recv_first(d):
        for e in ((1,) if d == 0 else (0, 1)):
            pltpu.make_async_remote_copy(
                src_ref=piece(d, e), dst_ref=piece(d, e), send_sem=s1.at[e, d], recv_sem=r1.at[e, d],
                device_id=twin, device_id_type=MESH).wait_recv()

    def relay(ref, d, e, device, start):
        cp = pltpu.make_async_remote_copy(
            src_ref=ref, dst_ref=ref, send_sem=s1.at[e, d], recv_sem=r1.at[e, d],
            device_id=device, device_id_type=MESH)
        if start:
            cp.start()
            later.append(cp)
        else:
            cp.wait_recv()

    def relayed(d):
        if d == 4:
            relay(piece(4, 0), 4, 0, near[2], False)
            relay(piece(4, 1), 4, 1, near[6], False)
        else:
            relay(both(d), d, 0, near[1 if d == 3 else 7], False)

    later = []
    for i, d in enumerate(ORDER):
        if d == 0:
            for k in range(8):
                weights(k)
        if d == 3:
            tables()
            for k in range(8, KT):
                weights(k)
        if d == 0:
            mine.wait()
        if d in (3, 4, 5):
            relayed(d)
        else:
            recv_first(d)
        if d == 2:
            relay(both(2), 3, 0, near[1], True)
            relay(piece(2, 0), 4, 0, near[2], True)
        if d == 6:
            relay(both(6), 5, 0, near[7], True)
            relay(piece(6, 1), 4, 1, near[6], True)
        zz = plane(d)
        part = g.at[pl.ds(zz * 2, 2), rows(c, pos)]
        for j in (2, 1, 3):
            cp = pltpu.make_async_remote_copy(
                src_ref=part, dst_ref=part, send_sem=s2.at[j, d], recv_sem=r2.at[j, d],
                device_id=ring[j], device_id_type=MESH)
            cp.start()
            later.append(cp)

    def half(d, c_):
        ref = g.at[pl.ds((z + 8 - d) % 8 * 2, 2), pl.ds(pl.multiple_of(c_ * 128, 128), 128)]
        return pltpu.make_async_remote_copy(
            src_ref=ref, dst_ref=ref, send_sem=s3.at[d], recv_sem=r3.at[d],
            device_id=twin, device_id_type=MESH)

    for d in ORDER:
        zz = (z + 8 - d) % 8
        for j in (1, 3, 2):
            part = g.at[pl.ds(zz * 2, 2), rows(c, (pos + 4 - j) % 4)]
            pltpu.make_async_remote_copy(
                src_ref=part, dst_ref=part, send_sem=s2.at[j, d], recv_sem=r2.at[j, d],
                device_id=ring[j], device_id_type=MESH).wait_recv()
        later.append(half(d, c))
        later[-1].start()
    for d in ORDER:
        half(d, 1 - c).wait_recv()
    for cp in first + later:
        cp.wait_send()


def gather(row, cd, airr, own, amp, integ):
    smem = pl.BlockSpec(memory_space=pltpu.SMEM)
    vmem = pl.BlockSpec(memory_space=pltpu.VMEM)
    hbm = pl.BlockSpec(memory_space=pl.ANY)
    dma = pltpu.SemaphoreType.DMA
    return pl.pallas_call(
        gather_kernel,
        out_shape=(
            jax.ShapeDtypeStruct((GATHERED, SLOTS * 8, 128), F32),
            jax.ShapeDtypeStruct((KT, 128, 256), BF16),
            jax.ShapeDtypeStruct((8, 128), jnp.int32),
            jax.ShapeDtypeStruct((1,), jnp.int32),
        ),
        in_specs=[smem, smem, smem, vmem, vmem, hbm, hbm],
        out_specs=(vmem, vmem, vmem, smem),
        scratch_shapes=[
            pltpu.VMEM((SLOTS * 8, 128), F32),
            pltpu.VMEM((1, 128), jnp.int32),
            pltpu.SMEM((1, 128), jnp.int32),
            pltpu.VMEM((IRREPS * VB // 8, 8, KT * CD_TILE), F32),
            pltpu.VMEM((OWN_TILES * KT, ROW_TILE, CD_TILE), F32),
            dma, dma, dma, dma, dma((2, 8)), dma((2, 8)), dma((4, 8)), dma((4, 8)), dma((8,)), dma((8,)),
        ],
        compiler_params=pltpu.CompilerParams(
            collective_id=0, has_side_effects=True, vmem_limit_bytes=24 * 2**20),
        name="gather",
    )(row, cd, airr, row.reshape(1, TILES), own, amp, integ)


def product_kernel(tab, g, w, p, acc):
    p[ZEROT] = jnp.zeros((8, 128), F32)

    def label(lab, c):
        first = tab[T_START, lab]
        nr = tab[T_START, lab + 1] - first
        nk = tab[T_NK, lab]

        def rowsof(m, c):
            tiles = []
            for t in range(MT):
                ok = m * MT + t < nr
                v = tab[T_LST, first + jnp.minimum(m * MT + t, nr - 1)]
                tiles.append((jnp.where(ok, v & 255, DUMPT), v >> 8))
            acc[...] = jnp.zeros_like(acc)

            def depth(kc, c):
                ks = [kc * KC + h for h in range(KC)]
                have = [k < nk for k in ks]
                cols = [tab[T_KL, lab * KT + jnp.where(ok, k, 0)] for ok, k in zip(have, ks)]
                at = [jnp.where(ok, k, 0) for ok, k in zip(have, ks)]
                parts = []
                for h in range(KC):
                    part = jnp.concatenate([g[tiles[t][1] + at[h]] for t in range(MT)], axis=0)
                    parts.append(part if h == 0 else jnp.where(have[h], part, 0.0))
                a = jnp.concatenate(parts, axis=1)
                hi = a.astype(BF16)
                lo = (a - hi.astype(F32)).astype(BF16)
                ww = jnp.concatenate([w[k] for k in cols], axis=0)
                big = jnp.dot(hi, ww, preferred_element_type=F32)
                small = jnp.dot(lo, ww[:, :128], preferred_element_type=F32)
                acc[...] += big[:, :128] + (big[:, 128:] + small)
                return c

            lax.fori_loop(0, (nk + KC - 1) // KC, depth, 0)
            for t in range(MT):
                p[tiles[t][0]] = acc[t * 8:(t + 1) * 8, :]
            return c

        return lax.fori_loop(0, (nr + MT - 1) // MT, rowsof, c)

    lax.fori_loop(0, IRREPS, label, 0)


def product(tab, g, w):
    smem = pl.BlockSpec(memory_space=pltpu.SMEM)
    vmem = pl.BlockSpec(memory_space=pltpu.VMEM)
    return pl.pallas_call(
        product_kernel,
        out_shape=jax.ShapeDtypeStruct((PT, 8, 128), F32),
        in_specs=[smem, vmem, vmem],
        out_specs=vmem,
        scratch_shapes=[pltpu.VMEM((MT * 8, 128), F32)],
        compiler_params=pltpu.CompilerParams(vmem_limit_bytes=24 * 2**20),
        name="product",
    )(tab, g, w)


def owners_kernel(tab, p, out, send, loc_sem, ss, rs):
    me = lax.axis_index("slab")
    c = me % 2
    y = (me // 2) % 4
    xl = me // 8
    steps = [(a, b, e) for a, b in ((1, 2), (0, 2), (1, 1), (1, 3), (0, 1), (0, 3), (1, 0)) for e in (0, 1)] + [(0, 0, 1)]
    targets = [(xl + a) % 2 * 8 + (y + b) % 4 * 2 + (c + e) % 2 for a, b, e in steps]
    sources = [(xl + a) % 2 * 8 + (y + 4 - b) % 4 * 2 + (c + e) % 2 for a, b, e in steps]
    barrier = pltpu.get_barrier_semaphore()
    for o in targets:
        pl.semaphore_signal(barrier, inc=1, device_id={"slab": o}, device_id_type=MESH)

    def make(i, o):
        block = jnp.concatenate([p[tab[T_SRC + o // 8, o % 8 * CAP + q]] for q in range(CAP)], axis=0)
        send[i] = jnp.transpose(block)[:SENT]

    def copy(i, o, place):
        return pltpu.make_async_remote_copy(
            src_ref=send.at[i], dst_ref=out.at[place], send_sem=ss.at[i], recv_sem=rs.at[i],
            device_id={"slab": o}, device_id_type=MESH)

    EARLY = 4
    copies = []
    for i, o in enumerate(targets):
        make(i, o)
        if i == EARLY - 1:
            pl.semaphore_wait(barrier, 15)
            for j in range(EARLY):
                copies.append(copy(j, targets[j], me))
                copies[-1].start()
        elif i >= EARLY:
            copies.append(copy(i, o, me))
            copies[-1].start()
    make(15, me)
    local = pltpu.make_async_copy(send.at[15], out.at[me], loc_sem)
    local.start()
    for i, o in enumerate(sources):
        copy(i, o, o).wait_recv()
    for cp in copies:
        cp.wait_send()
    local.wait()


def owners(tab, p):
    smem = pl.BlockSpec(memory_space=pltpu.SMEM)
    vmem = pl.BlockSpec(memory_space=pltpu.VMEM)
    dma = pltpu.SemaphoreType.DMA
    return pl.pallas_call(
        owners_kernel,
        out_shape=jax.ShapeDtypeStruct((16, SENT, 128), F32),
        in_specs=[smem, vmem],
        out_specs=vmem,
        scratch_shapes=[pltpu.VMEM((16, SENT, 128), F32), dma, dma((16,)), dma((16,))],
        compiler_params=pltpu.CompilerParams(
            collective_id=1, has_side_effects=True, vmem_limit_bytes=24 * 2**20),
        name="owners",
    )(tab, p)


def expand_kernel(airr, tab, arrived, out, stage, sems):
    blk = lax.axis_index("blk")
    lab = tab[T_LAB:T_LAB + 1, :]
    upper = lax.broadcasted_iota(jnp.int32, (8, 128), 0) < 4

    def one(s, c):
        want = lab ^ airr[s, blk]
        block = arrived[s]
        block = jnp.concatenate([block, block[0:4]], axis=0)
        moved = jnp.concatenate([block[100:104], block[0:100]], axis=0)
        for m in range(IRREPS // 2):
            even = want == 2 * m
            odd = want == 2 * m + 1
            base = 2 * VB * m
            stage[s, base:base + 96, :] = jnp.where(even, block[:96], 0.0)
            stage[s, base + 96:base + 104, :] = jnp.where(
                upper, jnp.where(even, block[96:], 0.0), jnp.where(odd, moved[:8], 0.0))
            stage[s, base + 104:base + 200, :] = jnp.where(odd, moved[8:], 0.0)
        pltpu.make_async_copy(stage.at[s], out.at[s], sems.at[s]).start()
        return c

    lax.fori_loop(0, 16, one, 0, unroll=4)
    for s in range(16):
        pltpu.make_async_copy(stage.at[s], out.at[s], sems.at[s]).wait()


def expand(airr, tab, arrived):
    return pl.pallas_call(
        expand_kernel,
        out_shape=jax.ShapeDtypeStruct((16, IRREPS * VB, 128), F32),
        in_specs=[pl.BlockSpec(memory_space=pltpu.SMEM)] + [pl.BlockSpec(memory_space=pltpu.VMEM)] * 2,
        out_specs=pl.BlockSpec(memory_space=pl.ANY),
        scratch_shapes=[pltpu.VMEM((16, IRREPS * VB, 128), F32), pltpu.SemaphoreType.DMA((16,))],
        compiler_params=pltpu.CompilerParams(vmem_limit_bytes=40 * 2**20),
        name="expand",
    )(airr, tab, arrived)


def dense(amplitude, integ, row, cd, airr, owner):
    slab = lax.axis_index("slab")
    blk = lax.axis_index("blk")
    own_a = airr[slab, blk]
    copies = jnp.broadcast_to(amplitude[None], (16,) + amplitude.shape)
    piece = lax.all_to_all(copies, "blk", split_axis=0, concat_axis=0, tiled=True).reshape(-1, KT * CD_TILE)
    cd_cols = jnp.repeat(cd, CD_TILE)
    labels = jnp.repeat(row, ROW_TILE)
    coupled = jnp.where(labels[:, None] == cd_cols[None, :], piece, 0.0)
    blocks = integ.reshape(IRREPS, VB, KT * CD_TILE)
    want = cd_cols ^ own_a
    kept = jnp.sum(jnp.where(want[None, None, :] == jnp.arange(IRREPS)[:, None, None], blocks, 0.0), axis=0)
    prod = jnp.dot(coupled, kept.T, precision=lax.Precision.HIGHEST, preferred_element_type=F32)
    prod = jnp.concatenate([prod.reshape(TILES, ROW_TILE, VB), jnp.zeros((1, ROW_TILE, VB), F32)], axis=0)
    own = owner[:, 0]
    tiles = jnp.arange(TILES, dtype=jnp.int32)
    ahead = (own[:, None] == own[None, :]) & (tiles[None, :] < tiles[:, None])
    target = own * CAP + jnp.sum(ahead.astype(jnp.int32), axis=1)
    hit = target[None, :] == jnp.arange(16 * CAP, dtype=jnp.int32)[:, None]
    source = ZEROT + jnp.sum(jnp.where(hit, tiles[None, :] - ZEROT, 0), axis=1)
    packed = jnp.take(prod, source, axis=0).reshape(16, CAP * ROW_TILE, VB)
    arrived = lax.all_to_all(packed, "slab", split_axis=0, concat_axis=0, tiled=True)
    arrived = jnp.transpose(arrived, (0, 2, 1))
    return arrived


def shards(amplitude, integrals, row, cd, airr, owner):
    integ = integrals.reshape(KT * CD_TILE, IRREPS * VB).T
    amp = amplitude.reshape(OWN_TILES, ROW_TILE, KT, CD_TILE).transpose(0, 2, 1, 3)
    g, w, tab, fit = gather(
        row, cd, airr, owner.reshape(1, TILES), amp.reshape(OWN_TILES * KT, ROW_TILE, CD_TILE),
        integ.reshape(IRREPS * VB // 8, 8, KT * CD_TILE))

    p = product(tab, g.reshape(GATHERED * SLOTS, 8, 128), w)

    def fast(amplitude, integ, row, cd, airr, owner, tab, p):
        return owners(tab, p)

    def slow(amplitude, integ, row, cd, airr, owner, tab, p):
        return dense(amplitude, integ, row, cd, airr, owner)

    arrived = lax.cond(fit[0] == 1, fast, slow, amplitude, integ, row, cd, airr, owner, tab, p)
    out = expand(airr, tab, arrived)
    return jnp.transpose(out, (2, 0, 1)).reshape(CAP * ROW_TILE, 16, 1, IRREPS * VB)


def solution(mesh):
    return jax.shard_map(
        shards,
        mesh=mesh,
        in_specs=(P("blk", None), P(None, "slab", "blk", None), P(), P(), P(), P()),
        out_specs=P("slab", None, "blk", None),
        check_vma=False,
    )
```
